32 devices in a mesh: seq: 8 (over z, y), slide: 4 (over x, core).
Axes of the slice: x: 2, y: 2, z: 4, core: 2. Of those that a mesh axis runs over, the one named last changes fastest.
Arguments:
- tile_embed: bfloat16 [4096, 1536], P(('seq', 'slide')), may hold values from -6 to 6
- destination: int32 [4096], P(('seq', 'slide')), may hold values from 0 to 4095, as said below
- slide_lengths: int32 [4], replicated, may hold values from 32 to 2048, as said below
- w_inner: bfloat16 [1536, 3072], replicated, may hold values from -0.15625 to 0.15625
- w_gate: bfloat16 [1536, 3072], replicated, may hold values from -0.15625 to 0.15625
- conv_weight: float32 [2, 4, 3072], replicated, may hold values from -2 to 2
- conv_bias: float32 [2, 3072], replicated, may hold values from -2 to 2
- x_project: bfloat16 [2, 3072, 128], replicated, may hold values from -0.109375 to 0.109375
- dt_project: bfloat16 [2, 96, 3072], replicated, may hold values from -0.625 to 0.625
- dt_bias: float32 [2, 3072], replicated, may hold values from -6 to -3.5
- decay: float32 [2, 16, 3072], replicated, may hold values from 0.009765625 to 32
- skip_gain: float32 [2, 3072], replicated, may hold values from 0.5 to 1.5
Outputs:
- mixed: bfloat16 [4096, 3072], P(('seq', 'slide'))
The draws below stay inside these ranges and needn't reach their ends.
Inputs may be any that keep to these rules, and one draw needn't show every extreme that they name: `destination`: a permutation; the tile in row b of the 128 rows of each encoder device has a packed position from b * 32 to (b + 1) * 32 - 1. `slide_lengths`: each a multiple of 32; they sum to 4096; the longest is exactly 2048.
All inputs are finite; a program needn't handle non-finite values.
Results may differ from the reference program's by a relative error of at most 0.0067.
Values may be sent and summed in bfloat16 or wider, within the bound.
A program may use at most 320 MiB of HBM per device.

```python
import jax
import jax.numpy as jnp
from jax import lax

D = 1536
E = 3072
N = 16
R_DT = 96
KCONV = 4
ROWS = 128
SHARDS = 32
TILES = 4096
SEQ_CAP = 2048
SLIDES = 4


def draw_destination(key, part):
    keys = jax.random.split(key, ROWS)
    orders = jax.vmap(lambda one_key: jax.random.permutation(one_key, SHARDS))(keys)
    base = (jnp.arange(ROWS, dtype=jnp.int32) * SHARDS)[:, None]
    return (base + orders.astype(jnp.int32)).T.reshape(-1)


def draw_slide_lengths(key, part):
    units = ROWS // 2
    first_key = jax.random.fold_in(key, 11)
    second_key = jax.random.fold_in(key, 23)
    cuts = jnp.sort(jax.random.permutation(first_key, units - 1)[:SLIDES - 2].astype(jnp.int32) + 1)
    edges = jnp.concatenate([jnp.zeros((1,), jnp.int32), cuts, jnp.full((1,), units, jnp.int32)])
    pieces = edges[1:] - edges[:-1]
    longest = jax.random.randint(second_key, (), 0, SLIDES)
    slide_ids = jnp.arange(SLIDES, dtype=jnp.int32)
    others = jnp.clip(slide_ids - (slide_ids > longest).astype(jnp.int32), 0, SLIDES - 2)
    values = jnp.where(slide_ids == longest, units, pieces[others])
    return (values * SHARDS).astype(jnp.int32)


def draw_decay(key, part):
    order_keys = jax.random.split(jax.random.fold_in(key, 31), 2)
    pick_key = jax.random.fold_in(key, 37)
    fast_key = jax.random.fold_in(key, 41)
    slow_key = jax.random.fold_in(key, 43)
    orders = jax.vmap(lambda one_key: jax.random.permutation(one_key, E))(order_keys)
    slow_channel = orders.astype(jnp.int32) < E // 2
    slow_state = jax.random.randint(pick_key, (2, E), 0, N)
    state_ids = jnp.arange(N, dtype=jnp.int32)
    slow_mask = slow_channel[:, None, :] & (state_ids[None, :, None] == slow_state[:, None, :])
    fast_log = jax.random.uniform(fast_key, (2, N, E), jnp.float32, 0.0, jnp.log(32.0))
    slow_log = jax.random.uniform(slow_key, (2, N, E), jnp.float32, jnp.log(20.0 / SEQ_CAP), jnp.log(150.0 / SEQ_CAP))
    return jnp.where(slow_mask, jnp.exp(slow_log), jnp.exp(fast_log)).astype(jnp.float32)


def levels(stream_key, shape, cuts, least, high):
    loudness, own = 1.0, jax.random.fold_in(stream_key, 6)
    for position, parts in cuts:
        steps = jnp.exp(jax.random.uniform(jax.random.fold_in(own, position), (parts,), jnp.float32, least / len(cuts), high / len(cuts)))
        loudness = loudness * jnp.repeat(steps, shape[position] // parts).reshape([-1 if axis == position else 1 for axis in range(len(shape))])
    return loudness


def scatter_about(own_key, extent, deviation, limit, cuts=(), held_as=jnp.bfloat16):
    factor_of = levels(own_key, extent, cuts, -0.22, 0.18) if cuts else 1.0
    result = jax.random.normal(own_key, extent, jnp.float32) * deviation * factor_of
    return jnp.minimum(jnp.maximum(result, -limit), limit).astype(held_as)


def setup_inputs(seed: int = 0) -> dict:
    streams_of = jax.random.split(jax.random.key(seed), 13)
    return {
        "tile_embed": scatter_about(streams_of[0], (TILES, D), 1.0, 6.0, ((0, 32),)),
        "destination": draw_destination(jax.random.fold_in(streams_of[12], 71), 0),
        "slide_lengths": draw_slide_lengths(jax.random.fold_in(streams_of[12], 71), 0),
        "w_inner": scatter_about(streams_of[3], (D, E), D ** -0.5, 0.15625),
        "w_gate": scatter_about(streams_of[4], (D, E), D ** -0.5, 0.15625),
        "conv_weight": scatter_about(streams_of[5], (2, KCONV, E), 0.5, 2.0, (), jnp.float32),
        "conv_bias": scatter_about(streams_of[6], (2, E), 0.5, 2.0, (), jnp.float32),
        "x_project": scatter_about(streams_of[7], (2, E, R_DT + 2 * N), E ** -0.5, 0.109375),
        "dt_project": scatter_about(streams_of[8], (2, R_DT, E), R_DT ** -0.5, 0.625),
        "dt_bias": jnp.clip(jax.random.uniform(streams_of[9], (2, E), jnp.float32, -6.0, -3.5), -6.0, -3.5),
        "decay": draw_decay(jax.random.fold_in(streams_of[12], 71), 0),
        "skip_gain": jnp.clip(jax.random.uniform(streams_of[11], (2, E), jnp.float32, 0.5, 1.5), 0.5, 1.5),
    }


def sweep(step_size, mixed_in, b_rows, c_rows, rates, skip, reverse):
    def row_step(hidden, row_data):
        dt_row, u_row, b_row, c_row = row_data
        hidden = jnp.exp(dt_row[None, :] * rates) * hidden + (dt_row * u_row)[None, :] * b_row[:, None]
        return hidden, jnp.sum(c_row[:, None] * hidden, axis=0)

    start = jnp.zeros(rates.shape, jnp.float32)
    _, outputs = lax.scan(row_step, start, (step_size, mixed_in, b_rows, c_rows), reverse=reverse)
    return outputs + skip[None, :] * mixed_in


def direction(mixed_in, x_proj, dt_proj, bias, rates, skip, reverse):
    rank = dt_proj.shape[0]
    states = rates.shape[0]
    project = jnp.dot(mixed_in, x_proj, preferred_element_type=jnp.float32)
    low = project[:, :rank].astype(jnp.bfloat16)
    b_rows = project[:, rank:rank + states]
    c_rows = project[:, rank + states:]
    step_size = jax.nn.softplus(jnp.dot(low, dt_proj, preferred_element_type=jnp.float32) + bias[None, :])
    return sweep(step_size, mixed_in.astype(jnp.float32), b_rows, c_rows, rates, skip, reverse)


def reference(tile_embed, destination, slide_lengths, w_inner, w_gate, conv_weight, conv_bias, x_project, dt_project, dt_bias, decay, skip_gain):
    tiles = tile_embed.shape[0]
    width = w_inner.shape[1]
    taps = conv_weight.shape[1]
    projected = jnp.dot(tile_embed, w_inner, preferred_element_type=jnp.float32).astype(jnp.bfloat16)
    packed = jnp.zeros((tiles + SEQ_CAP, width), jnp.bfloat16).at[destination].set(projected)
    offsets = (jnp.cumsum(slide_lengths) - slide_lengths).astype(jnp.int32)
    positions = jnp.arange(SEQ_CAP, dtype=jnp.int32)
    results = jnp.zeros((tiles + SEQ_CAP, width), jnp.bfloat16)
    for slide in range(SLIDES):
        start = offsets[slide].astype(jnp.int32)
        valid = (positions < slide_lengths[slide])[:, None]
        window = lax.dynamic_slice_in_dim(packed, start, SEQ_CAP, 0)
        window = jnp.where(valid, window, jnp.zeros_like(window))
        padded = jnp.pad(window, ((taps - 1, taps - 1), (0, 0)))
        forward_sum = conv_bias[0][None, :]
        backward_sum = conv_bias[1][None, :]
        for tap in range(taps):
            forward_sum = forward_sum + conv_weight[0, tap][None, :] * padded[tap:tap + SEQ_CAP].astype(jnp.float32)
            lead = 2 * (taps - 1) - tap
            backward_sum = backward_sum + conv_weight[1, tap][None, :] * padded[lead:lead + SEQ_CAP].astype(jnp.float32)
        u_fwd = jnp.where(valid, jax.nn.silu(forward_sum), 0.0).astype(jnp.bfloat16)
        u_bwd = jnp.where(valid, jax.nn.silu(backward_sum), 0.0).astype(jnp.bfloat16)
        y_fwd = direction(u_fwd, x_project[0], dt_project[0], dt_bias[0], -decay[0], skip_gain[0], False)
        y_bwd = direction(u_bwd, x_project[1], dt_project[1], dt_bias[1], -decay[1], skip_gain[1], True)
        total = (y_fwd + y_bwd).astype(jnp.bfloat16)
        current = lax.dynamic_slice_in_dim(results, start, SEQ_CAP, 0)
        results = lax.dynamic_update_slice_in_dim(results, current + jnp.where(valid, total, jnp.zeros_like(total)), start, 0)
    gathered = results[destination]
    gate = jnp.dot(tile_embed, w_gate, preferred_element_type=jnp.float32)
    return (gathered.astype(jnp.float32) * jax.nn.silu(gate)).astype(jnp.bfloat16)
```

```python
import functools

import jax
import jax.numpy as jnp
from jax import lax
from jax.experimental import pallas as pl
from jax.experimental.pallas import tpu as pltpu
from jax.sharding import PartitionSpec as P

AXES = ("seq", "slide")
LANES = 128
SUB = 8
LOG2E = 1.4426950408889634


def slide_starts(len_ref):
    starts = [jnp.int32(0)]
    for s in range(len_ref.shape[0]):
        starts.append(starts[-1] + len_ref[s])
    return starts


def keep_at(starts, pos):
    hit = pos == starts[0]
    for s in starts[1:]:
        hit = jnp.logical_or(hit, pos == s)
    return jnp.where(hit, 0.0, 1.0).astype(jnp.float32)


def spread_rates(decay_ref, rate_scr, folds):
    count = decay_ref.shape[0]
    for k in range(folds):
        rate_scr[pl.ds(k, count, stride=folds), :] = (
            decay_ref[:, k * LANES : (k + 1) * LANES] * -LOG2E
        )


def sweep_kernel(
    states, rank, chunk,
    me_ref, len_ref, inner_ref, prev_ref, next_ref, cw_ref, cb_ref, xp_ref, dp_ref, db_ref,
    decay_ref, skip_ref,
    dt_ref, proj_ref, y_ref, pay_ref,
    pad, u_ref, rate_scr, ubf, bc, sem,
):
    rows, width = inner_ref.shape
    folds = width // LANES
    taps = cw_ref.shape[0] // 2
    halo = prev_ref.shape[0]
    starts = slide_starts(len_ref)
    base = me_ref[0] * rows
    spread_rates(decay_ref, rate_scr, folds)
    pad[0:SUB, :] = prev_ref[...].astype(jnp.float32)
    pad[SUB : SUB + rows, :] = inner_ref[...].astype(jnp.float32)
    pad[SUB + rows : 2 * SUB + rows, :] = next_ref[...].astype(jnp.float32)
    where_at = base + lax.broadcasted_iota(jnp.int32, (rows, LANES), 0)
    masks = {}
    for dist in range(1, taps):
        for sign in (-1, 1):
            bad = jnp.zeros((rows, LANES), jnp.bool_)
            for s in starts:
                if sign < 0:
                    bad = bad | ((where_at - dist < s) & (where_at >= s))
                else:
                    bad = bad | ((where_at < s) & (where_at + dist >= s))
            masks[sign * dist] = jnp.where(bad, 0.0, 1.0)
    block = LANES
    wide = 2 * LANES
    for d in range(2):
        acc = jnp.zeros((rows, LANES), jnp.float32)
        for cb in range(width // wide):
            for half in range(2):
                k = 2 * cb + half
                cols = slice(k * block, (k + 1) * block)
                total = jnp.broadcast_to(cb_ref[d : d + 1, cols], (rows, block))
                for tap in range(taps):
                    dist = (tap - (taps - 1)) if d == 0 else (taps - 1 - tap)
                    term = pad[SUB + dist : SUB + dist + rows, cols]
                    if dist != 0:
                        term = term * masks[dist]
                    total = total + cw_ref[d * taps + tap : d * taps + tap + 1, cols] * term
                u = (total / (1.0 + jnp.exp(-total))).astype(jnp.bfloat16)
                ubf[:, cols] = u
                u_ref[d, pl.ds(k, rows, stride=folds), :] = u.astype(jnp.float32)
            wcols = slice(cb * wide, (cb + 1) * wide)
            acc = acc + jnp.dot(
                ubf[:, wcols], xp_ref[d, wcols, :], preferred_element_type=jnp.float32
            )
        proj_ref[d * rows : (d + 1) * rows, :] = acc
        low = acc[:, :rank].astype(jnp.bfloat16)
        for cb in range(width // wide):
            wcols = slice(cb * wide, (cb + 1) * wide)
            v = jnp.dot(low, dp_ref[d, :, wcols], preferred_element_type=jnp.float32)
            v = v + db_ref[d : d + 1, wcols]
            step = jnp.maximum(v, 0.0) + jnp.log1p(jnp.exp(-jnp.abs(v)))
            for half in range(2):
                dt_ref[d, pl.ds(2 * cb + half, rows, stride=folds), :] = step[
                    :, half * LANES : (half + 1) * LANES
                ]
    copy = pltpu.make_async_copy(proj_ref, bc, sem)
    copy.start()
    copy.wait()
    chunks = rows // chunk
    zero = jnp.zeros((SUB, LANES), jnp.float32)
    for d in range(2):
        for j in range(folds // SUB):
            rates = [
                rate_scr[(d * states + n) * folds + j * SUB : (d * states + n) * folds + (j + 1) * SUB, :]
                for n in range(states)
            ]
            skip = skip_ref[d, j * SUB : (j + 1) * SUB, :]

            def chunk_step(ci, carry):
                hs, sdt = carry
                c = ci if d == 0 else chunks - 1 - ci
                keep = keep_at(starts, base + (c if d == 0 else c + 1) * chunk)
                hs = tuple(h * keep for h in hs)

                def row_step(i, inner_carry):
                    hs, sdt = inner_carry
                    t = c * chunk + (i if d == 0 else chunk - 1 - i)
                    spot = pl.ds(pl.multiple_of(t * folds + j * SUB, SUB), SUB)
                    dt = dt_ref[d, spot, :]
                    u = u_ref[d, spot, :]
                    dtu = dt * u
                    parts = [skip * u, None, None, None]
                    out = []
                    for n in range(states):
                        h = jnp.exp2(dt * rates[n]) * hs[n] + dtu * bc[d * rows + t, rank + n]
                        out.append(h)
                        term = h * bc[d * rows + t, rank + states + n]
                        q = n % 4
                        parts[q] = term if parts[q] is None else parts[q] + term
                    y = (parts[0] + parts[1]) + (parts[2] + parts[3])
                    if d == 0:
                        y_ref[spot, :] = y
                    else:
                        y_ref[spot, :] += y
                    return (tuple(out), sdt + dt)

                return lax.fori_loop(0, chunk, row_step, (hs, sdt), unroll=2)

            hs, sdt = lax.fori_loop(0, chunks, chunk_step, ((zero,) * states, zero))
            for n in range(states):
                pay_ref[d * states + n, j * SUB : (j + 1) * SUB, :] = hs[n]
                pay_ref[d * states + n, folds + j * SUB : folds + (j + 1) * SUB, :] = sdt


def relay_kernel(states, split, rows, chunk, me_ref, len_ref, got_ref, rate_ref, out_ref):
    shards = got_ref.shape[0]
    depth = got_ref.shape[1] // 2
    starts = slide_starts(len_ref)
    backward = me_ref[0] // split >= states
    rate = rate_ref[...] * -LOG2E

    def step(i, h):
        s = jnp.where(backward, shards - 1 - i, i)
        keep = jnp.float32(1.0)
        for c in range(rows // chunk):
            keep = keep * keep_at(
                starts, s * rows + c * chunk + jnp.where(backward, chunk, 0)
            )
        out_ref[s] = h.astype(jnp.bfloat16)
        got = got_ref[s].astype(jnp.float32)
        return jnp.exp2(rate * got[depth:]) * (h * keep) + got[:depth]

    lax.fori_loop(0, shards, step, jnp.zeros((depth, LANES), jnp.float32))


def finish_kernel(
    states, rank, chunk,
    me_ref, len_ref, bc, dt_ref, y_ref, enter_ref, decay_ref, slot_ref,
    out_ref,
    rate_scr, tot,
):
    rows, width = out_ref.shape
    folds = width // LANES
    chunks = rows // chunk
    starts = slide_starts(len_ref)
    base = me_ref[0] * rows
    spread_rates(decay_ref, rate_scr, folds)
    for d in range(2):
        for j in range(folds // SUB):
            rates = [
                rate_scr[(d * states + n) * folds + j * SUB : (d * states + n) * folds + (j + 1) * SUB, :]
                for n in range(states)
            ]
            enters = [
                enter_ref[d * states + n, j * SUB : (j + 1) * SUB, :].astype(jnp.float32)
                for n in range(states)
            ]

            def chunk_step(ci, carry):
                alive, sdt = carry
                c = ci if d == 0 else chunks - 1 - ci
                alive = alive * keep_at(starts, base + (c if d == 0 else c + 1) * chunk)

                def row_step(i, sdt):
                    t = c * chunk + (i if d == 0 else chunk - 1 - i)
                    spot = pl.ds(pl.multiple_of(t * folds + j * SUB, SUB), SUB)
                    sdt = sdt + dt_ref[d, spot, :]
                    parts = [None] * 4
                    for n in range(states):
                        term = jnp.exp2(sdt * rates[n]) * (
                            enters[n] * bc[d * rows + t, rank + states + n]
                        )
                        q = n % 4
                        parts[q] = term if parts[q] is None else parts[q] + term
                    y = ((parts[0] + parts[1]) + (parts[2] + parts[3])) * alive
                    if d == 0:
                        tot[spot, :] = y_ref[spot, :] + y
                    else:
                        tot[spot, :] += y
                    return sdt

                return (alive, lax.fori_loop(0, chunk, row_step, sdt, unroll=2))

            lax.fori_loop(
                0, chunks, chunk_step, (jnp.float32(1.0), jnp.zeros((SUB, LANES), jnp.float32))
            )
    pick = (
        slot_ref[...] == lax.broadcasted_iota(jnp.int32, (rows, rows), 1)
    ).astype(jnp.bfloat16)
    for k in range(folds):
        part = tot[pl.ds(k, rows, stride=folds), :].astype(jnp.bfloat16)
        out_ref[:, k * LANES : (k + 1) * LANES] = jnp.dot(
            pick, part, preferred_element_type=jnp.float32
        ).astype(jnp.bfloat16)


def local(
    tile_embed, destination, slide_lengths, w_inner, w_gate, conv_weight, conv_bias, x_project,
    dt_project, dt_bias, decay, skip_gain,
):
    shards = lax.axis_size(AXES)
    rows, model = tile_embed.shape
    width = w_inner.shape[1]
    states = decay.shape[1]
    rank = dt_project.shape[1]
    taps = conv_weight.shape[1]
    folds = width // LANES
    per_peer = rows // shards
    chunk = min(shards, rows)
    split = shards // (2 * states)
    halo = taps - 1
    me = lax.axis_index(AXES).astype(jnp.int32)
    me_arr = me[None]
    f32, bf16 = jnp.float32, jnp.bfloat16
    vmem = pl.BlockSpec(memory_space=pltpu.VMEM)
    smem = pl.BlockSpec(memory_space=pltpu.SMEM)
    params = pltpu.CompilerParams(vmem_limit_bytes=48 * 1024 * 1024)

    slot_col = jnp.broadcast_to((destination % rows).astype(bf16)[:, None], (rows, LANES))
    sent = jnp.concatenate([tile_embed, slot_col], axis=1).reshape(shards, per_peer, model + LANES)
    got = lax.all_to_all(sent, AXES, split_axis=0, concat_axis=0, tiled=True)
    got = got.reshape(rows, model + LANES)
    slot = got[:, model].astype(jnp.int32)
    place = (slot[None, :] == jnp.arange(rows, dtype=jnp.int32)[:, None]).astype(bf16)
    ordered = jnp.dot(place, got[:, :model], preferred_element_type=f32).astype(bf16)
    inner = jnp.dot(ordered, w_inner, preferred_element_type=f32).astype(bf16)
    up = [(i, i + 1) for i in range(shards - 1)]
    down = [(i + 1, i) for i in range(shards - 1)]
    before = lax.ppermute(inner[rows - SUB :], AXES, up)
    after = lax.ppermute(inner[:SUB], AXES, down)
    dt, proj, y, pay = pl.pallas_call(
        functools.partial(sweep_kernel, states, rank, chunk),
        out_shape=(
            jax.ShapeDtypeStruct((2, rows * folds, LANES), f32),
            jax.ShapeDtypeStruct((2 * rows, LANES), f32),
            jax.ShapeDtypeStruct((rows * folds, LANES), f32),
            jax.ShapeDtypeStruct((2 * states, 2 * folds, LANES), f32),
        ),
        in_specs=[smem, smem] + [vmem] * 10,
        out_specs=(vmem,) * 4,
        scratch_shapes=[
            pltpu.VMEM((rows + 2 * SUB, width), f32),
            pltpu.VMEM((2, rows * folds, LANES), f32),
            pltpu.VMEM((2 * states * folds, LANES), f32),
            pltpu.VMEM((rows, width), bf16),
            pltpu.SMEM((2 * rows, LANES), f32),
            pltpu.SemaphoreType.DMA,
        ],
        compiler_params=params,
        name="sweep",
    )(
        me_arr, slide_lengths, inner, before, after, conv_weight.reshape(2 * taps, width), conv_bias,
        x_project, dt_project, dt_bias, decay.reshape(2 * states, width),
        skip_gain.reshape(2, folds, LANES),
    )
    pay = pay.astype(bf16).reshape(2 * states, 2, split, folds // split, LANES)
    pay = pay.swapaxes(1, 2).reshape(shards, 2 * folds // split, LANES)
    theirs = lax.all_to_all(pay, AXES, split_axis=0, concat_axis=0, tiled=True)
    my_rate = lax.dynamic_slice_in_dim(
        decay.reshape(shards, folds // split, LANES), me, 1, axis=0
    )[0]
    enter = pl.pallas_call(
        functools.partial(relay_kernel, states, split, rows, chunk),
        out_shape=jax.ShapeDtypeStruct((shards, folds // split, LANES), bf16),
        in_specs=[smem, smem, vmem, vmem],
        out_specs=vmem,
        compiler_params=params,
        name="relay",
    )(me_arr, slide_lengths, theirs, my_rate)
    enter = lax.all_to_all(enter, AXES, split_axis=0, concat_axis=0, tiled=True)
    enter = enter.reshape(2 * states, folds, LANES)
    back = pl.pallas_call(
        functools.partial(finish_kernel, states, rank, chunk),
        out_shape=jax.ShapeDtypeStruct((rows, width), bf16),
        in_specs=[smem, smem, smem] + [vmem] * 5,
        out_specs=vmem,
        scratch_shapes=[
            pltpu.VMEM((2 * states * folds, LANES), f32),
            pltpu.VMEM((rows * folds, LANES), f32),
        ],
        compiler_params=params,
        name="finish",
    )(
        me_arr, slide_lengths, proj, dt, y, enter, decay.reshape(2 * states, width),
        slot[:, None],
    )
    back = back.reshape(shards, per_peer, width)
    returned = lax.all_to_all(back, AXES, split_axis=0, concat_axis=0, tiled=True)
    gate = jnp.dot(tile_embed, w_gate, preferred_element_type=f32)
    return (returned.reshape(rows, width).astype(f32) * jax.nn.silu(gate)).astype(bf16)


def solution(mesh):
    placed = (P(AXES, None), P(AXES)) + (P(),) * 10
    return jax.shard_map(
        local, mesh=mesh, in_specs=placed, out_specs=P(AXES, None), check_vma=False
    )
```

```python
import functools

import jax
import jax.numpy as jnp
from jax import lax
from jax.experimental import pallas as pl
from jax.experimental.pallas import tpu as pltpu
from jax.sharding import PartitionSpec as P

AXES = ("seq", "slide")
LANES = 128
SUB = 8
LOG2E = 1.4426950408889634


def slide_starts(len_ref):
    starts = [jnp.int32(0)]
    for s in range(len_ref.shape[0]):
        starts.append(starts[-1] + len_ref[s])
    return starts


def keep_at(starts, pos):
    hit = pos == starts[0]
    for s in starts[1:]:
        hit = jnp.logical_or(hit, pos == s)
    return jnp.where(hit, 0.0, 1.0).astype(jnp.float32)


def spread_rates(decay_ref, rate_scr, folds):
    count = decay_ref.shape[0]
    for k in range(folds):
        rate_scr[pl.ds(k, count, stride=folds), :] = (
            decay_ref[:, k * LANES : (k + 1) * LANES] * -LOG2E
        )


def sweep_kernel(
    states, rank, chunk,
    me_ref, len_ref, inner_ref, prev_ref, next_ref, cw_ref, cb_ref, xp_ref, dp_ref, db_ref,
    decay_ref, skip_ref,
    dt_ref, proj_ref, y_ref, pay_ref,
    pad, u_ref, rate_scr, ubf, held, bc, sem,
):
    rows, width = inner_ref.shape
    folds = width // LANES
    taps = cw_ref.shape[0] // 2
    halo = prev_ref.shape[0]
    starts = slide_starts(len_ref)
    base = me_ref[0] * rows
    spread_rates(decay_ref, rate_scr, folds)
    pad[0:SUB, :] = prev_ref[halo - SUB :, :].astype(jnp.float32)
    pad[SUB : SUB + rows, :] = inner_ref[...].astype(jnp.float32)
    pad[SUB + rows : 2 * SUB + rows, :] = next_ref[0:SUB, :].astype(jnp.float32)
    where_at = base + lax.broadcasted_iota(jnp.int32, (rows, LANES), 0)
    masks = {}
    for dist in range(1, taps):
        for sign in (-1, 1):
            bad = jnp.zeros((rows, LANES), jnp.bool_)
            for s in starts:
                if sign < 0:
                    bad = bad | ((where_at - dist < s) & (where_at >= s))
                else:
                    bad = bad | ((where_at < s) & (where_at + dist >= s))
            masks[sign * dist] = jnp.where(bad, 0.0, 1.0)
    block = LANES
    wide = 2 * LANES
    for d in range(2):
        acc = jnp.zeros((rows, LANES), jnp.float32)
        for cb in range(width // wide):
            for half in range(2):
                k = 2 * cb + half
                cols = slice(k * block, (k + 1) * block)
                total = jnp.broadcast_to(cb_ref[d : d + 1, cols], (rows, block))
                for tap in range(taps):
                    dist = (tap - (taps - 1)) if d == 0 else (taps - 1 - tap)
                    term = pad[SUB + dist : SUB + dist + rows, cols]
                    if dist != 0:
                        term = term * masks[dist]
                    total = total + cw_ref[d * taps + tap : d * taps + tap + 1, cols] * term
                u = (total / (1.0 + jnp.exp(-total))).astype(jnp.bfloat16)
                ubf[:, cols] = u
                u_ref[d, pl.ds(k, rows, stride=folds), :] = u.astype(jnp.float32)
            wcols = slice(cb * wide, (cb + 1) * wide)
            acc = acc + jnp.dot(
                ubf[:, wcols], xp_ref[d, wcols, :], preferred_element_type=jnp.float32
            )
        proj_ref[d * rows : (d + 1) * rows, :] = acc
        low = acc[:, :rank].astype(jnp.bfloat16)
        for cb in range(width // wide):
            wcols = slice(cb * wide, (cb + 1) * wide)
            v = jnp.dot(low, dp_ref[d, :, wcols], preferred_element_type=jnp.float32)
            v = v + db_ref[d : d + 1, wcols]
            step = jnp.maximum(v, 0.0) + jnp.log1p(jnp.exp(-jnp.abs(v)))
            for half in range(2):
                dt_ref[d, pl.ds(2 * cb + half, rows, stride=folds), :] = step[
                    :, half * LANES : (half + 1) * LANES
                ]
    copy = pltpu.make_async_copy(proj_ref, bc, sem)
    copy.start()
    copy.wait()
    chunks = rows // chunk
    zero = jnp.zeros((SUB, LANES), jnp.float32)
    for d in range(2):
        for j in range(folds // SUB):
            rates = [
                rate_scr[(d * states + n) * folds + j * SUB : (d * states + n) * folds + (j + 1) * SUB, :]
                for n in range(states)
            ]
            skip = skip_ref[d, j * SUB : (j + 1) * SUB, :]

            def chunk_step(ci, carry):
                hs, sdt = carry
                c = ci if d == 0 else chunks - 1 - ci
                keep = keep_at(starts, base + (c if d == 0 else c + 1) * chunk)
                hs = tuple(h * keep for h in hs)

                def row_step(i, inner_carry):
                    hs, sdt = inner_carry
                    t = c * chunk + (i if d == 0 else chunk - 1 - i)
                    spot = pl.ds(pl.multiple_of(t * folds + j * SUB, SUB), SUB)
                    dt = dt_ref[d, spot, :]
                    u = u_ref[d, spot, :]
                    dtu = dt * u
                    parts = [skip * u, None, None, None]
                    out = []
                    for n in range(states):
                        h = jnp.exp2(dt * rates[n]) * hs[n] + dtu * bc[d * rows + t, rank + n]
                        out.append(h)
                        term = h * bc[d * rows + t, rank + states + n]
                        q = n % 4
                        parts[q] = term if parts[q] is None else parts[q] + term
                    y = (parts[0] + parts[1]) + (parts[2] + parts[3])
                    if d == 0:
                        y_ref[spot, :] = y
                    else:
                        y_ref[spot, :] += y
                    return (tuple(out), sdt + dt)

                return lax.fori_loop(0, chunk, row_step, (hs, sdt), unroll=2)

            hs, sdt = lax.fori_loop(0, chunks, chunk_step, ((zero,) * states, zero))
            for n in range(states):
                held[d * states + n, j * SUB : (j + 1) * SUB, :] = hs[n]
                held[d * states + n, folds + j * SUB : folds + (j + 1) * SUB, :] = sdt
    pay_ref[...] = held[...].astype(jnp.bfloat16)


def relay_kernel(states, split, rows, chunk, me_ref, len_ref, got_ref, rate_ref, out_ref):
    shards = got_ref.shape[0]
    depth = got_ref.shape[1] // 2
    starts = slide_starts(len_ref)
    backward = me_ref[0] // split >= states
    rate = rate_ref[...] * -LOG2E

    def step(i, h):
        s = jnp.where(backward, shards - 1 - i, i)
        keep = jnp.float32(1.0)
        for c in range(rows // chunk):
            keep = keep * keep_at(
                starts, s * rows + c * chunk + jnp.where(backward, chunk, 0)
            )
        out_ref[s] = h.astype(jnp.bfloat16)
        got = got_ref[s].astype(jnp.float32)
        return jnp.exp2(rate * got[depth:]) * (h * keep) + got[:depth]

    lax.fori_loop(0, shards, step, jnp.zeros((depth, LANES), jnp.float32))


def finish_kernel(
    states, rank, chunk,
    me_ref, len_ref, bc, dt_ref, y_ref, enter_ref, decay_ref, place_ref,
    out_ref,
    rate_scr, tot,
):
    rows = place_ref.shape[0]
    folds = decay_ref.shape[1] // LANES
    chunks = rows // chunk
    starts = slide_starts(len_ref)
    base = me_ref[0] * rows
    spread_rates(decay_ref, rate_scr, folds)
    for d in range(2):
        for j in range(folds // SUB):
            rates = [
                rate_scr[(d * states + n) * folds + j * SUB : (d * states + n) * folds + (j + 1) * SUB, :]
                for n in range(states)
            ]
            enters = [
                enter_ref[d * states + n, j * SUB : (j + 1) * SUB, :].astype(jnp.float32)
                for n in range(states)
            ]

            def chunk_step(ci, carry):
                alive, sdt = carry
                c = ci if d == 0 else chunks - 1 - ci
                alive = alive * keep_at(starts, base + (c if d == 0 else c + 1) * chunk)

                def row_step(i, sdt):
                    t = c * chunk + (i if d == 0 else chunk - 1 - i)
                    spot = pl.ds(pl.multiple_of(t * folds + j * SUB, SUB), SUB)
                    sdt = sdt + dt_ref[d, spot, :]
                    parts = [None] * 4
                    for n in range(states):
                        term = jnp.exp2(sdt * rates[n]) * (
                            enters[n] * bc[d * rows + t, rank + states + n]
                        )
                        q = n % 4
                        parts[q] = term if parts[q] is None else parts[q] + term
                    y = ((parts[0] + parts[1]) + (parts[2] + parts[3])) * alive
                    if d == 0:
                        tot[spot, :] = y_ref[spot, :] + y
                    else:
                        tot[spot, :] += y
                    return sdt

                return (alive, lax.fori_loop(0, chunk, row_step, sdt, unroll=2))

            lax.fori_loop(
                0, chunks, chunk_step, (jnp.float32(1.0), jnp.zeros((SUB, LANES), jnp.float32))
            )
    pick = place_ref[...]
    for k in range(folds):
        part = tot[pl.ds(k, rows, stride=folds), :].astype(jnp.bfloat16)
        tot[pl.ds(k, rows, stride=folds), :] = lax.dot_general(
            pick, part, (((0,), (0,)), ((), ())), preferred_element_type=jnp.float32
        )
    out_ref[...] = tot[...].astype(jnp.bfloat16)


def peer_id(peer):
    count = lax.axis_size("slide")
    return {"seq": lax.div(peer, count), "slide": lax.rem(peer, count)}


def greet_all(shards, me):
    barrier = pltpu.get_barrier_semaphore()

    def greet(i, _):
        pl.semaphore_signal(
            barrier, inc=1, device_id=peer_id(lax.rem(me + i, shards)),
            device_id_type=pl.DeviceIdType.MESH,
        )
        return 0

    lax.fori_loop(1, shards, greet, 0)
    pl.semaphore_wait(barrier, shards - 1)


def block_copy(src, dst, i, me, shards, send_sem, recv_sem):
    peer = lax.rem(me + i, shards)
    return pltpu.make_async_remote_copy(
        src_ref=src.at[peer], dst_ref=dst.at[me], send_sem=send_sem.at[i],
        recv_sem=recv_sem.at[i], device_id=peer_id(peer),
        device_id_type=pl.DeviceIdType.MESH,
    )


def block_landed(src, dst, i, me, shards, send_sem, recv_sem):
    peer = lax.rem(me + i, shards)
    origin = lax.rem(me + shards - i, shards)
    return pltpu.make_async_remote_copy(
        src_ref=src.at[peer], dst_ref=dst.at[origin], send_sem=send_sem.at[i],
        recv_sem=recv_sem.at[i], device_id=peer_id(peer),
        device_id_type=pl.DeviceIdType.MESH,
    )


def start_blocks(*args):
    src, dst, me, shards, send_sem, recv_sem = args

    def go(i, _):
        block_copy(src, dst, i, me, shards, send_sem, recv_sem).start()
        return 0

    lax.fori_loop(1, shards, go, 0)


def await_blocks(*args):
    src, dst, me, shards, send_sem, recv_sem = args

    def stop(i, _):
        block_landed(src, dst, i, me, shards, send_sem, recv_sem).wait()
        return 0

    lax.fori_loop(1, shards, stop, 0)


def arrive_kernel(
    shards, emb_ref, slots_ref, wg_ref, wi_ref,
    inner_ref, prev_ref, next_ref, gate_ref, place_ref,
    scr, send, got, gslot, ordered, wg, wi,
    send_sem, recv_sem, slot_send, slot_recv, halo_send, halo_recv, load_sem,
):
    rows, model = emb_ref.shape
    width = inner_ref.shape[1]
    folds = model // LANES
    wide = 2 * LANES
    edge = prev_ref.shape[0]
    me = lax.axis_index(AXES)
    load_gate = pltpu.make_async_copy(wg_ref, wg, load_sem.at[0])
    load_inner = pltpu.make_async_copy(wi_ref, wi, load_sem.at[1])
    load_gate.start()
    load_inner.start()
    for k in range(folds):
        scr[pl.ds(k, rows, stride=folds), :] = emb_ref[:, k * LANES : (k + 1) * LANES].astype(
            jnp.float32
        )
    send[...] = scr[...].astype(jnp.bfloat16).reshape(send.shape)
    greet_all(shards, me)
    start_blocks(slots_ref, gslot, me, shards, slot_send, slot_recv)
    start_blocks(send, got, me, shards, send_sem, recv_sem)
    got[me] = send[me]
    gslot[me] = slots_ref[me]
    load_gate.wait()

    def gate_tile(cb, _):
        cols = pl.ds(pl.multiple_of(cb * wide, wide), wide)
        v = jnp.dot(emb_ref[...], wg[:, cols], preferred_element_type=jnp.float32)
        gate_ref[:, cols] = v / (1.0 + jnp.exp(-v))
        return 0

    lax.fori_loop(0, width // wide, gate_tile, 0)
    load_inner.wait()
    await_blocks(slots_ref, gslot, me, shards, slot_send, slot_recv)
    await_blocks(send, got, me, shards, send_sem, recv_sem)
    slot_row = jnp.sum(gslot[...], axis=0)
    place = (
        jnp.broadcast_to(slot_row, (rows, rows))
        == lax.broadcasted_iota(jnp.int32, (rows, rows), 0).astype(jnp.float32)
    ).astype(jnp.bfloat16)
    place_ref[...] = place
    scr[...] = got[...].astype(jnp.float32).reshape(scr.shape)
    for k in range(folds):
        ordered[:, k * LANES : (k + 1) * LANES] = jnp.dot(
            place, scr[pl.ds(k, rows, stride=folds), :].astype(jnp.bfloat16),
            preferred_element_type=jnp.float32,
        ).astype(jnp.bfloat16)

    def inner_tile(cb, _):
        cols = pl.ds(pl.multiple_of(cb * wide, wide), wide)
        inner_ref[:, cols] = jnp.dot(
            ordered[...], wi[:, cols], preferred_element_type=jnp.float32
        ).astype(jnp.bfloat16)
        return 0

    lax.fori_loop(0, width // wide, inner_tile, 0)
    after = pltpu.make_async_remote_copy(
        src_ref=inner_ref.at[pl.ds(rows - edge, edge)], dst_ref=prev_ref,
        send_sem=halo_send.at[0], recv_sem=halo_recv.at[0],
        device_id=peer_id(lax.rem(me + 1, shards)), device_id_type=pl.DeviceIdType.MESH,
    )
    before = pltpu.make_async_remote_copy(
        src_ref=inner_ref.at[pl.ds(0, edge)], dst_ref=next_ref,
        send_sem=halo_send.at[1], recv_sem=halo_recv.at[1],
        device_id=peer_id(lax.rem(me + shards - 1, shards)), device_id_type=pl.DeviceIdType.MESH,
    )
    after.start()
    before.start()
    after.wait()
    before.wait()


def pass_kernel(
    shards, states, rows, chunk, len_ref, pay_ref, rate_ref,
    out_ref,
    got, ent, send_a, recv_a, send_b, recv_b,
):
    depth = rate_ref.shape[0]
    me = lax.axis_index(AXES)
    greet_all(shards, me)
    start_blocks(pay_ref, got, me, shards, send_a, recv_a)
    got[me] = pay_ref[me]
    starts = slide_starts(len_ref)
    back = lax.div(me, states)
    rate = rate_ref[...] * -LOG2E
    await_blocks(pay_ref, got, me, shards, send_a, recv_a)
    ent[...] = jnp.zeros(ent.shape, ent.dtype)

    def step(i, h):
        s = i + back * (shards - 1 - 2 * i)
        keep = jnp.float32(1.0)
        for c in range(rows // chunk):
            keep = keep * keep_at(starts, s * rows + c * chunk + back * chunk)
        ent[s, 0:depth, :] = h.astype(jnp.bfloat16)
        blk = got[s].astype(jnp.float32)
        return jnp.exp2(rate * blk[depth:]) * (h * keep) + blk[:depth]

    lax.fori_loop(0, shards, step, jnp.zeros((depth, LANES), jnp.float32))
    start_blocks(ent, out_ref, me, shards, send_b, recv_b)
    out_ref[me] = ent[me]
    await_blocks(ent, out_ref, me, shards, send_b, recv_b)


def return_kernel(shards, back_ref, gate_ref, out_ref, got, scr, send_sem, recv_sem):
    rows, width = out_ref.shape
    folds = width // LANES
    me = lax.axis_index(AXES)
    greet_all(shards, me)
    start_blocks(back_ref, got, me, shards, send_sem, recv_sem)
    got[me] = back_ref[me]
    await_blocks(back_ref, got, me, shards, send_sem, recv_sem)
    scr[...] = got[...].astype(jnp.float32).reshape(scr.shape)
    for k in range(folds):
        cols = slice(k * LANES, (k + 1) * LANES)
        out_ref[:, cols] = (
            scr[pl.ds(k, rows, stride=folds), :] * gate_ref[:, cols]
        ).astype(jnp.bfloat16)


def local(
    tile_embed, destination, slide_lengths, w_inner, w_gate, conv_weight, conv_bias, x_project,
    dt_project, dt_bias, decay, skip_gain,
):
    shards = lax.axis_size(AXES)
    rows, model = tile_embed.shape
    width = w_inner.shape[1]
    states = decay.shape[1]
    rank = dt_project.shape[1]
    taps = conv_weight.shape[1]
    folds = width // LANES
    per_peer = rows // shards
    chunk = min(shards, rows)
    split = shards // (2 * states)
    halo = taps - 1
    me = lax.axis_index(AXES).astype(jnp.int32)
    me_arr = me[None]
    f32, bf16 = jnp.float32, jnp.bfloat16
    vmem = pl.BlockSpec(memory_space=pltpu.VMEM)
    smem = pl.BlockSpec(memory_space=pltpu.SMEM)
    params = pltpu.CompilerParams(vmem_limit_bytes=48 * 1024 * 1024)

    any_space = pl.BlockSpec(memory_space=pl.ANY)
    mfolds = model // LANES
    fast = shards == 2 * states and (per_peer * mfolds) % 16 == 0 and (per_peer * folds) % 16 == 0
    dma = pltpu.SemaphoreType.DMA((shards,))

    def remote_params(number):
        return pltpu.CompilerParams(
            vmem_limit_bytes=48 * 1024 * 1024, collective_id=number, has_side_effects=True
        )

    if fast:
        lane = jnp.arange(rows, dtype=jnp.int32)[None, :]
        slots = jnp.tile((destination % rows).astype(f32).reshape(shards, per_peer), (1, shards))
        slots = jnp.where(lane // per_peer == me, slots, 0.0)[:, None, :]
        inner, before, after, gate, place = pl.pallas_call(
            functools.partial(arrive_kernel, shards),
            out_shape=(
                jax.ShapeDtypeStruct((rows, width), bf16),
                jax.ShapeDtypeStruct((2 * SUB, width), bf16),
                jax.ShapeDtypeStruct((2 * SUB, width), bf16),
                jax.ShapeDtypeStruct((rows, width), f32),
                jax.ShapeDtypeStruct((rows, rows), bf16),
            ),
            in_specs=[vmem, vmem, any_space, any_space],
            out_specs=(vmem,) * 5,
            scratch_shapes=[
                pltpu.VMEM((rows * mfolds, LANES), f32),
                pltpu.VMEM((shards, per_peer * mfolds, LANES), bf16),
                pltpu.VMEM((shards, per_peer * mfolds, LANES), bf16),
                pltpu.VMEM((shards, 1, rows), f32),
                pltpu.VMEM((rows, model), bf16),
                pltpu.VMEM((model, width), bf16),
                pltpu.VMEM((model, width), bf16),
                dma, dma, dma, dma,
                pltpu.SemaphoreType.DMA((2,)),
                pltpu.SemaphoreType.DMA((2,)),
                pltpu.SemaphoreType.DMA((2,)),
            ],
            compiler_params=remote_params(1),
            name="arrive",
        )(tile_embed, slots, w_gate, w_inner)
    else:
        slot_col = jnp.broadcast_to((destination % rows).astype(bf16)[:, None], (rows, LANES))
        sent = jnp.concatenate([tile_embed, slot_col], axis=1).reshape(shards, per_peer, model + LANES)
        got = lax.all_to_all(sent, AXES, split_axis=0, concat_axis=0, tiled=True)
        got = got.reshape(rows, model + LANES)
        slot = got[:, model].astype(jnp.int32)
        place = (slot[None, :] == jnp.arange(rows, dtype=jnp.int32)[:, None]).astype(bf16)
        ordered = jnp.dot(place, got[:, :model], preferred_element_type=f32).astype(bf16)
        inner = jnp.dot(ordered, w_inner, preferred_element_type=f32).astype(bf16)
        up = [(i, i + 1) for i in range(shards - 1)]
        down = [(i + 1, i) for i in range(shards - 1)]
        before = lax.ppermute(inner[rows - 2 * SUB :], AXES, up)
        after = lax.ppermute(inner[: 2 * SUB], AXES, down)
    dt, proj, y, pay = pl.pallas_call(
        functools.partial(sweep_kernel, states, rank, chunk),
        out_shape=(
            jax.ShapeDtypeStruct((2, rows * folds, LANES), f32),
            jax.ShapeDtypeStruct((2 * rows, LANES), f32),
            jax.ShapeDtypeStruct((rows * folds, LANES), f32),
            jax.ShapeDtypeStruct((2 * states, 2 * folds, LANES), bf16),
        ),
        in_specs=[smem, smem] + [vmem] * 10,
        out_specs=(vmem,) * 4,
        scratch_shapes=[
            pltpu.VMEM((rows + 2 * SUB, width), f32),
            pltpu.VMEM((2, rows * folds, LANES), f32),
            pltpu.VMEM((2 * states * folds, LANES), f32),
            pltpu.VMEM((rows, width), bf16),
            pltpu.VMEM((2 * states, 2 * folds, LANES), f32),
            pltpu.SMEM((2 * rows, LANES), f32),
            pltpu.SemaphoreType.DMA,
        ],
        compiler_params=params,
        name="sweep",
    )(
        me_arr, slide_lengths, inner, before, after, conv_weight.reshape(2 * taps, width), conv_bias,
        x_project, dt_project, dt_bias, decay.reshape(2 * states, width),
        skip_gain.reshape(2, folds, LANES),
    )
    if fast:
        my_rate = lax.dynamic_index_in_dim(decay.reshape(shards, width), me, 0, keepdims=False)
        enter = pl.pallas_call(
            functools.partial(pass_kernel, shards, states, rows, chunk),
            out_shape=jax.ShapeDtypeStruct((shards, 32, LANES), bf16),
            in_specs=[smem, vmem, vmem],
            out_specs=vmem,
            scratch_shapes=[
                pltpu.VMEM((shards, 2 * folds, LANES), bf16),
                pltpu.VMEM((shards, 32, LANES), bf16),
                dma, dma, dma, dma,
            ],
            compiler_params=remote_params(2),
            name="relay",
        )(slide_lengths, pay, my_rate.reshape(folds, LANES))
    else:
        pay = pay.reshape(2 * states, 2, split, folds // split, LANES)
        pay = pay.swapaxes(1, 2).reshape(shards, 2 * folds // split, LANES)
        theirs = lax.all_to_all(pay, AXES, split_axis=0, concat_axis=0, tiled=True)
        my_rate = lax.dynamic_slice_in_dim(
            decay.reshape(shards, folds // split, LANES), me, 1, axis=0
        )[0]
        enter = pl.pallas_call(
            functools.partial(relay_kernel, states, split, rows, chunk),
            out_shape=jax.ShapeDtypeStruct((shards, folds // split, LANES), bf16),
            in_specs=[smem, smem, vmem, vmem],
            out_specs=vmem,
            compiler_params=params,
            name="relay",
        )(me_arr, slide_lengths, theirs, my_rate)
        enter = lax.all_to_all(enter, AXES, split_axis=0, concat_axis=0, tiled=True)
        enter = enter.reshape(2 * states, folds, LANES)
    back = pl.pallas_call(
        functools.partial(finish_kernel, states, rank, chunk),
        out_shape=jax.ShapeDtypeStruct((rows * folds, LANES), bf16),
        in_specs=[smem, smem, smem] + [vmem] * 5,
        out_specs=vmem,
        scratch_shapes=[
            pltpu.VMEM((2 * states * folds, LANES), f32),
            pltpu.VMEM((rows * folds, LANES), f32),
        ],
        compiler_params=params,
        name="finish",
    )(
        me_arr, slide_lengths, proj, dt, y, enter, decay.reshape(2 * states, width),
        place,
    )
    if fast:
        return pl.pallas_call(
            functools.partial(return_kernel, shards),
            out_shape=jax.ShapeDtypeStruct((rows, width), bf16),
            in_specs=[vmem, vmem],
            out_specs=vmem,
            scratch_shapes=[
                pltpu.VMEM((shards, per_peer * folds, LANES), bf16),
                pltpu.VMEM((rows * folds, LANES), f32),
                dma, dma,
            ],
            compiler_params=remote_params(3),
            name="giveback",
        )(back.reshape(shards, per_peer * folds, LANES), gate)
    back = back.reshape(shards, per_peer, width)
    returned = lax.all_to_all(back, AXES, split_axis=0, concat_axis=0, tiled=True)
    gate = jnp.dot(tile_embed, w_gate, preferred_element_type=f32)
    return (returned.reshape(rows, width).astype(f32) * jax.nn.silu(gate)).astype(bf16)


def solution(mesh):
    placed = (P(AXES, None), P(AXES)) + (P(),) * 10
    return jax.shard_map(
        local, mesh=mesh, in_specs=placed, out_specs=P(AXES, None), check_vma=False
    )
```

```python
import functools

import jax
import jax.numpy as jnp
from jax import lax
from jax.experimental import pallas as pl
from jax.experimental.pallas import tpu as pltpu
from jax.sharding import PartitionSpec as P

AXES = ("seq", "slide")
LANES = 128
SUB = 8
LOG2E = 1.4426950408889634


def slide_starts(len_ref):
    starts = [jnp.int32(0)]
    for s in range(len_ref.shape[0]):
        starts.append(starts[-1] + len_ref[s])
    return starts


def keep_at(starts, pos):
    hit = pos == starts[0]
    for s in starts[1:]:
        hit = jnp.logical_or(hit, pos == s)
    return jnp.where(hit, 0.0, 1.0).astype(jnp.float32)


def spread_rates(decay_ref, rate_scr, folds):
    count = decay_ref.shape[0]
    for k in range(folds):
        rate_scr[pl.ds(k, count, stride=folds), :] = (
            decay_ref[:, k * LANES : (k + 1) * LANES] * -LOG2E
        )


def prepare(
    rank, starts, base, inner_ref, prev_ref, next_ref, cw_ref, cb_ref, xp_ref, dp_ref, db_ref,
    decay_ref, dt_ref, proj_ref, pad, u_ref, rate_scr, ubf, bc, sem,
):
    rows, width = inner_ref.shape
    folds = width // LANES
    taps = cw_ref.shape[0] // 2
    halo = prev_ref.shape[0]
    spread_rates(decay_ref, rate_scr, folds)
    pad[0:SUB, :] = prev_ref[halo - SUB :, :].astype(jnp.float32)
    pad[SUB : SUB + rows, :] = inner_ref[...].astype(jnp.float32)
    pad[SUB + rows : 2 * SUB + rows, :] = next_ref[0:SUB, :].astype(jnp.float32)
    where_at = base + lax.broadcasted_iota(jnp.int32, (rows, LANES), 0)
    masks = {}
    for dist in range(1, taps):
        for sign in (-1, 1):
            bad = jnp.zeros((rows, LANES), jnp.bool_)
            for s in starts:
                if sign < 0:
                    bad = bad | ((where_at - dist < s) & (where_at >= s))
                else:
                    bad = bad | ((where_at < s) & (where_at + dist >= s))
            masks[sign * dist] = jnp.where(bad, 0.0, 1.0)
    block = LANES
    wide = 2 * LANES
    for d in range(2):
        acc = jnp.zeros((rows, LANES), jnp.float32)
        for cb in range(width // wide):
            for half in range(2):
                k = 2 * cb + half
                cols = slice(k * block, (k + 1) * block)
                total = jnp.broadcast_to(cb_ref[d : d + 1, cols], (rows, block))
                for tap in range(taps):
                    dist = (tap - (taps - 1)) if d == 0 else (taps - 1 - tap)
                    term = pad[SUB + dist : SUB + dist + rows, cols]
                    if dist != 0:
                        term = term * masks[dist]
                    total = total + cw_ref[d * taps + tap : d * taps + tap + 1, cols] * term
                u = (total / (1.0 + jnp.exp(-total))).astype(jnp.bfloat16)
                ubf[:, cols] = u
                u_ref[d, pl.ds(k, rows, stride=folds), :] = u.astype(jnp.float32)
            wcols = slice(cb * wide, (cb + 1) * wide)
            acc = acc + jnp.dot(
                ubf[:, wcols], xp_ref[d, wcols, :], preferred_element_type=jnp.float32
            )
        proj_ref[d * rows : (d + 1) * rows, :] = acc
        low = acc[:, :rank].astype(jnp.bfloat16)
        for cb in range(width // wide):
            wcols = slice(cb * wide, (cb + 1) * wide)
            v = jnp.dot(low, dp_ref[d, :, wcols], preferred_element_type=jnp.float32)
            v = v + db_ref[d : d + 1, wcols]
            step = jnp.maximum(v, 0.0) + jnp.log1p(jnp.exp(-jnp.abs(v)))
            for half in range(2):
                dt_ref[d, pl.ds(2 * cb + half, rows, stride=folds), :] = step[
                    :, half * LANES : (half + 1) * LANES
                ]
    copy = pltpu.make_async_copy(proj_ref, bc, sem)
    copy.start()
    copy.wait()


def sweep_one(d, states, rank, chunk, rows, folds, starts, base, rate_scr, skip_ref, dt_ref, u_ref, bc, y_ref, keep_last):
    chunks = rows // chunk
    zero = jnp.zeros((SUB, LANES), jnp.float32)
    if True:
        for j in range(folds // SUB):
            rates = [
                rate_scr[(d * states + n) * folds + j * SUB : (d * states + n) * folds + (j + 1) * SUB, :]
                for n in range(states)
            ]
            skip = skip_ref[d, j * SUB : (j + 1) * SUB, :]

            def chunk_step(ci, carry):
                hs, sdt = carry
                c = ci if d == 0 else chunks - 1 - ci
                keep = keep_at(starts, base + (c if d == 0 else c + 1) * chunk)
                hs = tuple(h * keep for h in hs)

                def row_step(i, inner_carry):
                    hs, sdt = inner_carry
                    t = c * chunk + (i if d == 0 else chunk - 1 - i)
                    spot = pl.ds(pl.multiple_of(t * folds + j * SUB, SUB), SUB)
                    dt = dt_ref[d, spot, :]
                    u = u_ref[d, spot, :]
                    dtu = dt * u
                    parts = [skip * u, None, None, None]
                    out = []
                    for n in range(states):
                        h = jnp.exp2(dt * rates[n]) * hs[n] + dtu * bc[d * rows + t, rank + n]
                        out.append(h)
                        term = h * bc[d * rows + t, rank + states + n]
                        q = n % 4
                        parts[q] = term if parts[q] is None else parts[q] + term
                    y = (parts[0] + parts[1]) + (parts[2] + parts[3])
                    if d == 0:
                        y_ref[spot, :] = y
                    else:
                        y_ref[spot, :] += y
                    return (tuple(out), sdt + dt)

                return lax.fori_loop(0, chunk, row_step, (hs, sdt), unroll=2)

            hs, sdt = lax.fori_loop(0, chunks, chunk_step, ((zero,) * states, zero))
            keep_last(j, hs, sdt)


def sweep_kernel(
    states, rank, chunk,
    me_ref, len_ref, inner_ref, prev_ref, next_ref, cw_ref, cb_ref, xp_ref, dp_ref, db_ref,
    decay_ref, skip_ref,
    dt_ref, proj_ref, y_ref, pay_ref,
    pad, u_ref, rate_scr, ubf, held, bc, sem,
):
    rows, width = inner_ref.shape
    folds = width // LANES
    starts = slide_starts(len_ref)
    base = me_ref[0] * rows
    prepare(
        rank, starts, base, inner_ref, prev_ref, next_ref, cw_ref, cb_ref, xp_ref, dp_ref, db_ref,
        decay_ref, dt_ref, proj_ref, pad, u_ref, rate_scr, ubf, bc, sem,
    )
    for d in range(2):

        def keep_last(j, hs, sdt):
            for n in range(states):
                held[d * states + n, j * SUB : (j + 1) * SUB, :] = hs[n]
                held[d * states + n, folds + j * SUB : folds + (j + 1) * SUB, :] = sdt

        sweep_one(
            d, states, rank, chunk, rows, folds, starts, base, rate_scr, skip_ref, dt_ref, u_ref,
            bc, y_ref, keep_last,
        )
    pay_ref[...] = held[...].astype(jnp.bfloat16)


def relay_kernel(states, split, rows, chunk, me_ref, len_ref, got_ref, rate_ref, out_ref):
    shards = got_ref.shape[0]
    depth = got_ref.shape[1] // 2
    starts = slide_starts(len_ref)
    backward = me_ref[0] // split >= states
    rate = rate_ref[...] * -LOG2E

    def step(i, h):
        s = jnp.where(backward, shards - 1 - i, i)
        keep = jnp.float32(1.0)
        for c in range(rows // chunk):
            keep = keep * keep_at(
                starts, s * rows + c * chunk + jnp.where(backward, chunk, 0)
            )
        out_ref[s] = h.astype(jnp.bfloat16)
        got = got_ref[s].astype(jnp.float32)
        return jnp.exp2(rate * got[depth:]) * (h * keep) + got[:depth]

    lax.fori_loop(0, shards, step, jnp.zeros((depth, LANES), jnp.float32))


def finish_one(d, j, states, rank, chunk, rows, folds, starts, base, rate_scr, enter_of, dt_ref, bc, y_ref, tot):
    chunks = rows // chunk
    rates = [
        rate_scr[(d * states + n) * folds + j * SUB : (d * states + n) * folds + (j + 1) * SUB, :]
        for n in range(states)
    ]
    enters = [
        enter_of(n)
        for n in range(states)
    ]

    def chunk_step(ci, carry):
        alive, sdt = carry
        c = ci if d == 0 else chunks - 1 - ci
        alive = alive * keep_at(starts, base + (c if d == 0 else c + 1) * chunk)

        def row_step(i, sdt):
            t = c * chunk + (i if d == 0 else chunk - 1 - i)
            spot = pl.ds(pl.multiple_of(t * folds + j * SUB, SUB), SUB)
            sdt = sdt + dt_ref[d, spot, :]
            parts = [None] * 4
            for n in range(states):
                term = jnp.exp2(sdt * rates[n]) * (
                    enters[n] * bc[d * rows + t, rank + states + n]
                )
                q = n % 4
                parts[q] = term if parts[q] is None else parts[q] + term
            y = ((parts[0] + parts[1]) + (parts[2] + parts[3])) * alive
            if d == 0:
                tot[spot, :] = y_ref[spot, :] + y
            else:
                tot[spot, :] += y
            return sdt

        return (alive, lax.fori_loop(0, chunk, row_step, sdt, unroll=2))

    lax.fori_loop(
        0, chunks, chunk_step, (jnp.float32(1.0), jnp.zeros((SUB, LANES), jnp.float32))
    )


def finish_kernel(
    states, rank, chunk,
    me_ref, len_ref, bc, dt_ref, y_ref, enter_ref, decay_ref, place_ref,
    out_ref,
    rate_scr, tot,
):
    rows = place_ref.shape[0]
    folds = decay_ref.shape[1] // LANES
    starts = slide_starts(len_ref)
    base = me_ref[0] * rows
    spread_rates(decay_ref, rate_scr, folds)
    for d in range(2):
        for j in range(folds // SUB):

            def enter_of(n):
                return enter_ref[d * states + n, j * SUB : (j + 1) * SUB, :].astype(jnp.float32)

            finish_one(
                d, j, states, rank, chunk, rows, folds, starts, base, rate_scr, enter_of, dt_ref,
                bc, y_ref, tot,
            )
    pick = place_ref[...]
    for k in range(folds):
        part = tot[pl.ds(k, rows, stride=folds), :].astype(jnp.bfloat16)
        tot[pl.ds(k, rows, stride=folds), :] = lax.dot_general(
            pick, part, (((0,), (0,)), ((), ())), preferred_element_type=jnp.float32
        )
    out_ref[...] = tot[...].astype(jnp.bfloat16)


def peer_id(peer):
    count = lax.axis_size("slide")
    return {"seq": lax.div(peer, count), "slide": lax.rem(peer, count)}


def greet_all(shards, me):
    barrier = pltpu.get_barrier_semaphore()

    def greet(i, _):
        pl.semaphore_signal(
            barrier, inc=1, device_id=peer_id(lax.rem(me + i, shards)),
            device_id_type=pl.DeviceIdType.MESH,
        )
        return 0

    lax.fori_loop(1, shards, greet, 0)


def await_all(shards):
    pl.semaphore_wait(pltpu.get_barrier_semaphore(), shards - 1)


def block_copy(src, dst, i, me, shards, send_sem, recv_sem):
    peer = lax.rem(me + i, shards)
    return pltpu.make_async_remote_copy(
        src_ref=src.at[peer], dst_ref=dst.at[me], send_sem=send_sem.at[i],
        recv_sem=recv_sem.at[i], device_id=peer_id(peer),
        device_id_type=pl.DeviceIdType.MESH,
    )


def block_landed(src, dst, i, me, shards, send_sem, recv_sem):
    peer = lax.rem(me + i, shards)
    origin = lax.rem(me + shards - i, shards)
    return pltpu.make_async_remote_copy(
        src_ref=src.at[peer], dst_ref=dst.at[origin], send_sem=send_sem.at[i],
        recv_sem=recv_sem.at[i], device_id=peer_id(peer),
        device_id_type=pl.DeviceIdType.MESH,
    )


def start_blocks(*args):
    src, dst, me, shards, send_sem, recv_sem = args

    def go(i, _):
        block_copy(src, dst, i, me, shards, send_sem, recv_sem).start()
        return 0

    lax.fori_loop(1, shards, go, 0)


def await_blocks(*args):
    src, dst, me, shards, send_sem, recv_sem = args

    def stop(i, _):
        block_landed(src, dst, i, me, shards, send_sem, recv_sem).wait()
        return 0

    lax.fori_loop(1, shards, stop, 0)


def arrive_kernel(
    shards, emb_ref, slots_ref, wg_ref, wi_ref,
    inner_ref, prev_ref, next_ref, gate_ref, place_ref,
    scr, send, got, gslot, ordered, wg, wi,
    send_sem, recv_sem, slot_send, slot_recv, halo_send, halo_recv, load_sem,
):
    rows, model = emb_ref.shape
    width = inner_ref.shape[1]
    folds = model // LANES
    wide = 2 * LANES
    edge = prev_ref.shape[0]
    me = lax.axis_index(AXES)
    load_gate = pltpu.make_async_copy(wg_ref, wg, load_sem.at[0])
    load_inner = pltpu.make_async_copy(wi_ref, wi, load_sem.at[1])
    greet_all(shards, me)
    load_gate.start()
    load_inner.start()
    for k in range(folds):
        scr[pl.ds(k, rows, stride=folds), :] = emb_ref[:, k * LANES : (k + 1) * LANES].astype(
            jnp.float32
        )
    send[...] = scr[...].astype(jnp.bfloat16).reshape(send.shape)
    await_all(shards)
    start_blocks(slots_ref, gslot, me, shards, slot_send, slot_recv)
    start_blocks(send, got, me, shards, send_sem, recv_sem)
    got[me] = send[me]
    gslot[me] = slots_ref[me]
    load_gate.wait()

    def gate_tile(cb, _):
        cols = pl.ds(pl.multiple_of(cb * wide, wide), wide)
        v = jnp.dot(emb_ref[...], wg[:, cols], preferred_element_type=jnp.float32)
        gate_ref[:, cols] = v / (1.0 + jnp.exp(-v))
        return 0

    lax.fori_loop(0, width // wide, gate_tile, 0)
    load_inner.wait()
    await_blocks(slots_ref, gslot, me, shards, slot_send, slot_recv)
    await_blocks(send, got, me, shards, send_sem, recv_sem)
    slot_row = jnp.sum(gslot[...], axis=0)
    place = (
        jnp.broadcast_to(slot_row, (rows, rows))
        == lax.broadcasted_iota(jnp.int32, (rows, rows), 0).astype(jnp.float32)
    ).astype(jnp.bfloat16)
    place_ref[...] = place
    scr[...] = got[...].astype(jnp.float32).reshape(scr.shape)
    for k in range(folds):
        ordered[:, k * LANES : (k + 1) * LANES] = jnp.dot(
            place, scr[pl.ds(k, rows, stride=folds), :].astype(jnp.bfloat16),
            preferred_element_type=jnp.float32,
        ).astype(jnp.bfloat16)

    def inner_tile(cb, _):
        cols = pl.ds(pl.multiple_of(cb * wide, wide), wide)
        inner_ref[:, cols] = jnp.dot(
            ordered[...], wi[:, cols], preferred_element_type=jnp.float32
        ).astype(jnp.bfloat16)
        return 0

    lax.fori_loop(0, width // wide, inner_tile, 0)
    after = pltpu.make_async_remote_copy(
        src_ref=inner_ref.at[pl.ds(rows - edge, edge)], dst_ref=prev_ref,
        send_sem=halo_send.at[0], recv_sem=halo_recv.at[0],
        device_id=peer_id(lax.rem(me + 1, shards)), device_id_type=pl.DeviceIdType.MESH,
    )
    before = pltpu.make_async_remote_copy(
        src_ref=inner_ref.at[pl.ds(0, edge)], dst_ref=next_ref,
        send_sem=halo_send.at[1], recv_sem=halo_recv.at[1],
        device_id=peer_id(lax.rem(me + shards - 1, shards)), device_id_type=pl.DeviceIdType.MESH,
    )
    after.start()
    before.start()
    after.wait()
    before.wait()


def layer_kernel(
    shards, states, rank, chunk, groups,
    len_ref, inner_ref, prev_ref, next_ref, cw_ref, cb_ref, xp_ref, dp_ref, db_ref, decay_ref,
    skip_ref, myrate_ref, place_ref, gate_ref,
    out_ref,
    dt_ref, proj_ref, y_ref, pad, u_ref, rate_scr, ubf, held, bc, sem,
    stage, gotf, passes, pay0, pay1, got0, got1, ent0, ent1, land0, land1, enters,
    turn, back0, back1, back2, home0, home1, home2, send_sem, recv_sem,
):
    rows, width = inner_ref.shape
    folds = width // LANES
    per = folds // groups
    quads = shards // groups
    some = states // quads
    tall = some * per
    me = lax.axis_index(AXES)
    pays, gots, ents, lands = (pay0, pay1), (got0, got1), (ent0, ent1), (land0, land1)
    backs, homes = (back0, back1, back2), (home0, home1, home2)
    f32, bf16 = jnp.float32, jnp.bfloat16

    def route(src, dst, number):
        return (src, dst, me, shards, send_sem.at[number], recv_sem.at[number])

    greet_all(shards, me)
    starts = slide_starts(len_ref)
    base = me * rows
    prepare(
        rank, starts, base, inner_ref, prev_ref, next_ref, cw_ref, cb_ref, xp_ref, dp_ref, db_ref,
        decay_ref, dt_ref, proj_ref, pad, u_ref, rate_scr, ubf, bc, sem,
    )
    stage[...] = jnp.zeros(stage.shape, f32)
    passes[...] = jnp.zeros(passes.shape, f32)

    def keep_last(j, hs, sdt):
        for n in range(states):
            held[n * folds + j * SUB : n * folds + (j + 1) * SUB, :] = hs[n]
        held[states * folds + j * SUB : states * folds + (j + 1) * SUB, :] = sdt

    def sweep(d):
        sweep_one(
            d, states, rank, chunk, rows, folds, starts, base, rate_scr, skip_ref, dt_ref, u_ref,
            bc, y_ref, keep_last,
        )
        for g in range(groups):
            for q in range(quads):
                spot = (g * quads + q) * 2 * SUB
                for m in range(some):
                    row = (q * some + m) * folds + g * per
                    stage[spot + m * per : spot + (m + 1) * per, :] = held[row : row + per, :]
                row = states * folds + g * per
                stage[spot + tall : spot + tall + per, :] = held[row : row + per, :]
        pays[d][...] = stage[...].astype(bf16).reshape(pays[d].shape)

    def launch(d):
        start_blocks(*route(pays[d], gots[d], d))
        gots[d][me] = pays[d][me]

    def relay(d):
        await_blocks(*route(pays[d], gots[d], d))
        gotf[...] = gots[d][...].astype(f32)
        for m in range(some):
            rate = myrate_ref[d, m * per : (m + 1) * per, :] * -LOG2E
            passes[:, m * per : (m + 1) * per, :] = jnp.exp2(
                rate[None] * gotf[:, tall : tall + per, :]
            )

        def step(i, h):
            s = i if d == 0 else shards - 1 - i
            keep = jnp.float32(1.0)
            for c in range(rows // chunk):
                keep = keep * keep_at(starts, s * rows + c * chunk + d * chunk)
            ents[d][s] = h.astype(bf16)
            return passes[s] * (h * keep) + gotf[s]

        lax.fori_loop(0, shards, step, jnp.zeros((2 * SUB, LANES), f32))
        start_blocks(*route(ents[d], lands[d], 2 + d))
        lands[d][me] = ents[d][me]

    def arrive(d):
        await_blocks(*route(ents[d], lands[d], 2 + d))
        gotf[...] = lands[d][...].astype(f32)
        for g in range(groups):
            for q in range(quads):
                for m in range(some):
                    row = (q * some + m) * folds + g * per
                    enters[row : row + per, :] = gotf[g * quads + q, m * per : (m + 1) * per, :]

    def finish(d, j):
        def enter_of(n):
            return enters[n * folds + j * SUB : n * folds + (j + 1) * SUB, :]

        finish_one(
            d, j, states, rank, chunk, rows, folds, starts, base, rate_scr, enter_of, dt_ref, bc,
            y_ref, y_ref,
        )

    sweep(0)
    await_all(shards)
    launch(0)
    sweep(1)
    relay(0)
    launch(1)
    arrive(0)
    for j in range(folds // SUB):
        finish(0, j)
    relay(1)
    arrive(1)
    for j in range(folds // SUB):
        finish(1, j)
        for k in range(SUB):
            part = y_ref[pl.ds(j * SUB + k, rows, stride=folds), :].astype(bf16)
            turn[pl.ds(k, rows, stride=SUB), :] = lax.dot_general(
                place_ref[...], part, (((0,), (0,)), ((), ())), preferred_element_type=f32
            )
        backs[j][...] = turn[...].astype(bf16).reshape(backs[j].shape)
        start_blocks(*route(backs[j], homes[j], 4 + j))
        homes[j][me] = backs[j][me]
    for j in range(folds // SUB):
        await_blocks(*route(backs[j], homes[j], 4 + j))
        turn[...] = homes[j][...].astype(f32).reshape(turn.shape)
        for k in range(SUB):
            cols = slice((j * SUB + k) * LANES, (j * SUB + k + 1) * LANES)
            out_ref[:, cols] = (
                turn[pl.ds(k, rows, stride=SUB), :] * gate_ref[:, cols]
            ).astype(bf16)


def local(
    tile_embed, destination, slide_lengths, w_inner, w_gate, conv_weight, conv_bias, x_project,
    dt_project, dt_bias, decay, skip_gain,
):
    shards = lax.axis_size(AXES)
    rows, model = tile_embed.shape
    width = w_inner.shape[1]
    states = decay.shape[1]
    rank = dt_project.shape[1]
    taps = conv_weight.shape[1]
    folds = width // LANES
    per_peer = rows // shards
    chunk = min(shards, rows)
    split = shards // (2 * states)
    halo = taps - 1
    me = lax.axis_index(AXES).astype(jnp.int32)
    me_arr = me[None]
    f32, bf16 = jnp.float32, jnp.bfloat16
    vmem = pl.BlockSpec(memory_space=pltpu.VMEM)
    smem = pl.BlockSpec(memory_space=pltpu.SMEM)
    params = pltpu.CompilerParams(vmem_limit_bytes=60 * 1024 * 1024)

    any_space = pl.BlockSpec(memory_space=pl.ANY)
    mfolds = model // LANES
    groups = 8
    fast = (
        shards == 2 * states and shards % groups == 0 and folds == 3 * SUB
        and states % (shards // groups) == 0 and (per_peer * mfolds) % 16 == 0
        and (per_peer * SUB) % 16 == 0
    )
    dma = pltpu.SemaphoreType.DMA((shards,))

    def remote_params(number):
        return pltpu.CompilerParams(
            vmem_limit_bytes=60 * 1024 * 1024, collective_id=number, has_side_effects=True
        )

    if fast:
        lane = jnp.arange(rows, dtype=jnp.int32)[None, :]
        slots = jnp.tile((destination % rows).astype(f32).reshape(shards, per_peer), (1, shards))
        slots = jnp.where(lane // per_peer == me, slots, 0.0)[:, None, :]
        inner, before, after, gate, place = pl.pallas_call(
            functools.partial(arrive_kernel, shards),
            out_shape=(
                jax.ShapeDtypeStruct((rows, width), bf16),
                jax.ShapeDtypeStruct((2 * SUB, width), bf16),
                jax.ShapeDtypeStruct((2 * SUB, width), bf16),
                jax.ShapeDtypeStruct((rows, width), f32),
                jax.ShapeDtypeStruct((rows, rows), bf16),
            ),
            in_specs=[vmem, vmem, any_space, any_space],
            out_specs=(vmem,) * 5,
            scratch_shapes=[
                pltpu.VMEM((rows * mfolds, LANES), f32),
                pltpu.VMEM((shards, per_peer * mfolds, LANES), bf16),
                pltpu.VMEM((shards, per_peer * mfolds, LANES), bf16),
                pltpu.VMEM((shards, 1, rows), f32),
                pltpu.VMEM((rows, model), bf16),
                pltpu.VMEM((model, width), bf16),
                pltpu.VMEM((model, width), bf16),
                dma, dma, dma, dma,
                pltpu.SemaphoreType.DMA((2,)),
                pltpu.SemaphoreType.DMA((2,)),
                pltpu.SemaphoreType.DMA((2,)),
            ],
            compiler_params=remote_params(1),
            name="arrive",
        )(tile_embed, slots, w_gate, w_inner)
    else:
        slot_col = jnp.broadcast_to((destination % rows).astype(bf16)[:, None], (rows, LANES))
        sent = jnp.concatenate([tile_embed, slot_col], axis=1).reshape(shards, per_peer, model + LANES)
        got = lax.all_to_all(sent, AXES, split_axis=0, concat_axis=0, tiled=True)
        got = got.reshape(rows, model + LANES)
        slot = got[:, model].astype(jnp.int32)
        place = (slot[None, :] == jnp.arange(rows, dtype=jnp.int32)[:, None]).astype(bf16)
        ordered = jnp.dot(place, got[:, :model], preferred_element_type=f32).astype(bf16)
        inner = jnp.dot(ordered, w_inner, preferred_element_type=f32).astype(bf16)
        up = [(i, i + 1) for i in range(shards - 1)]
        down = [(i + 1, i) for i in range(shards - 1)]
        before = lax.ppermute(inner[rows - 2 * SUB :], AXES, up)
        after = lax.ppermute(inner[: 2 * SUB], AXES, down)
    if fast:
        quads = shards // groups
        mine = decay.reshape(2, quads, states // quads, groups, width // groups)
        mine = lax.dynamic_slice_in_dim(mine, lax.rem(me, quads), 1, axis=1)
        mine = lax.dynamic_slice_in_dim(mine, lax.div(me, quads), 1, axis=3)
        mine = mine.reshape(2, states // quads * (folds // groups), LANES)
        cell = pltpu.VMEM((shards, 2 * SUB, LANES), bf16)
        third = pltpu.VMEM((shards, per_peer * SUB, LANES), bf16)
        return pl.pallas_call(
            functools.partial(layer_kernel, shards, states, rank, chunk, groups),
            out_shape=jax.ShapeDtypeStruct((rows, width), bf16),
            in_specs=[smem] + [vmem] * 13,
            out_specs=vmem,
            scratch_shapes=[
                pltpu.VMEM((2, rows * folds, LANES), f32),
                pltpu.VMEM((2 * rows, LANES), f32),
                pltpu.VMEM((rows * folds, LANES), f32),
                pltpu.VMEM((rows + 2 * SUB, width), f32),
                pltpu.VMEM((2, rows * folds, LANES), f32),
                pltpu.VMEM((2 * states * folds, LANES), f32),
                pltpu.VMEM((rows, width), bf16),
                pltpu.VMEM(((states + 1) * folds, LANES), f32),
                pltpu.SMEM((2 * rows, LANES), f32),
                pltpu.SemaphoreType.DMA,
                pltpu.VMEM((shards * 2 * SUB, LANES), f32),
                pltpu.VMEM((shards, 2 * SUB, LANES), f32),
                pltpu.VMEM((shards, 2 * SUB, LANES), f32),
                cell, cell, cell, cell, cell, cell, cell, cell,
                pltpu.VMEM((states * folds, LANES), f32),
                pltpu.VMEM((rows * SUB, LANES), f32),
                third, third, third, third, third, third,
                pltpu.SemaphoreType.DMA((7, shards)),
                pltpu.SemaphoreType.DMA((7, shards)),
            ],
            compiler_params=remote_params(2),
            name="layer",
        )(
            slide_lengths, inner, before, after, conv_weight.reshape(2 * taps, width), conv_bias,
            x_project, dt_project, dt_bias, decay.reshape(2 * states, width),
            skip_gain.reshape(2, folds, LANES), mine, place, gate,
        )
    dt, proj, y, pay = pl.pallas_call(
        functools.partial(sweep_kernel, states, rank, chunk),
        out_shape=(
            jax.ShapeDtypeStruct((2, rows * folds, LANES), f32),
            jax.ShapeDtypeStruct((2 * rows, LANES), f32),
            jax.ShapeDtypeStruct((rows * folds, LANES), f32),
            jax.ShapeDtypeStruct((2 * states, 2 * folds, LANES), bf16),
        ),
        in_specs=[smem, smem] + [vmem] * 10,
        out_specs=(vmem,) * 4,
        scratch_shapes=[
            pltpu.VMEM((rows + 2 * SUB, width), f32),
            pltpu.VMEM((2, rows * folds, LANES), f32),
            pltpu.VMEM((2 * states * folds, LANES), f32),
            pltpu.VMEM((rows, width), bf16),
            pltpu.VMEM((2 * states, 2 * folds, LANES), f32),
            pltpu.SMEM((2 * rows, LANES), f32),
            pltpu.SemaphoreType.DMA,
        ],
        compiler_params=params,
        name="sweep",
    )(
        me_arr, slide_lengths, inner, before, after, conv_weight.reshape(2 * taps, width), conv_bias,
        x_project, dt_project, dt_bias, decay.reshape(2 * states, width),
        skip_gain.reshape(2, folds, LANES),
    )
    pay = pay.reshape(2 * states, 2, split, folds // split, LANES)
    pay = pay.swapaxes(1, 2).reshape(shards, 2 * folds // split, LANES)
    theirs = lax.all_to_all(pay, AXES, split_axis=0, concat_axis=0, tiled=True)
    my_rate = lax.dynamic_slice_in_dim(
        decay.reshape(shards, folds // split, LANES), me, 1, axis=0
    )[0]
    enter = pl.pallas_call(
        functools.partial(relay_kernel, states, split, rows, chunk),
        out_shape=jax.ShapeDtypeStruct((shards, folds // split, LANES), bf16),
        in_specs=[smem, smem, vmem, vmem],
        out_specs=vmem,
        compiler_params=params,
        name="relay",
    )(me_arr, slide_lengths, theirs, my_rate)
    enter = lax.all_to_all(enter, AXES, split_axis=0, concat_axis=0, tiled=True)
    enter = enter.reshape(2 * states, folds, LANES)
    back = pl.pallas_call(
        functools.partial(finish_kernel, states, rank, chunk),
        out_shape=jax.ShapeDtypeStruct((rows * folds, LANES), bf16),
        in_specs=[smem, smem, smem] + [vmem] * 5,
        out_specs=vmem,
        scratch_shapes=[
            pltpu.VMEM((2 * states * folds, LANES), f32),
            pltpu.VMEM((rows * folds, LANES), f32),
        ],
        compiler_params=params,
        name="finish",
    )(
        me_arr, slide_lengths, proj, dt, y, enter, decay.reshape(2 * states, width),
        place,
    )
    back = back.reshape(shards, per_peer, width)
    returned = lax.all_to_all(back, AXES, split_axis=0, concat_axis=0, tiled=True)
    gate = jnp.dot(tile_embed, w_gate, preferred_element_type=f32)
    return (returned.reshape(rows, width).astype(f32) * jax.nn.silu(gate)).astype(bf16)


def solution(mesh):
    placed = (P(AXES, None), P(AXES)) + (P(),) * 10
    return jax.shard_map(
        local, mesh=mesh, in_specs=placed, out_specs=P(AXES, None), check_vma=False
    )
```

```python
import functools

import jax
import jax.numpy as jnp
from jax import lax
from jax.experimental import pallas as pl
from jax.experimental.pallas import tpu as pltpu
from jax.sharding import PartitionSpec as P

AXES = ("seq", "slide")
LANES = 128
SUB = 8
LOG2E = 1.4426950408889634


def slide_starts(len_ref):
    starts = [jnp.int32(0)]
    for s in range(len_ref.shape[0]):
        starts.append(starts[-1] + len_ref[s])
    return starts


def keep_at(starts, pos):
    hit = pos == starts[0]
    for s in starts[1:]:
        hit = jnp.logical_or(hit, pos == s)
    return jnp.where(hit, 0.0, 1.0).astype(jnp.float32)


def spread_rates(decay_ref, rate_scr, folds):
    count = decay_ref.shape[1]
    for d in range(2):
        for k in range(folds):
            rate_scr[pl.ds(d * count * folds + k, count, stride=folds), :] = (
                decay_ref[d, :, k * LANES : (k + 1) * LANES] * -LOG2E
            )


def prepare(
    rank, starts, base, inner_ref, prev_ref, next_ref, cw_ref, cb_ref, xp_ref, dp_ref, db_ref,
    dt_ref, proj_ref, pad, u_ref, ubf, bc, sem,
):
    rows, width = inner_ref.shape
    folds = width // LANES
    taps = cw_ref.shape[1]
    halo = prev_ref.shape[0]
    pad[0:SUB, :] = prev_ref[halo - SUB :, :].astype(jnp.float32)
    pad[SUB : SUB + rows, :] = inner_ref[...].astype(jnp.float32)
    pad[SUB + rows : 2 * SUB + rows, :] = next_ref[0:SUB, :].astype(jnp.float32)
    where_at = base + lax.broadcasted_iota(jnp.int32, (rows, LANES), 0)
    masks = {}
    for dist in range(1, taps):
        for sign in (-1, 1):
            bad = jnp.zeros((rows, LANES), jnp.bool_)
            for s in starts:
                if sign < 0:
                    bad = bad | ((where_at - dist < s) & (where_at >= s))
                else:
                    bad = bad | ((where_at < s) & (where_at + dist >= s))
            masks[sign * dist] = jnp.where(bad, 0.0, 1.0)
    block = LANES
    wide = 2 * LANES
    for d in range(2):
        acc = jnp.zeros((rows, LANES), jnp.float32)
        for cb in range(width // wide):
            for half in range(2):
                k = 2 * cb + half
                cols = slice(k * block, (k + 1) * block)
                total = jnp.broadcast_to(cb_ref[d : d + 1, cols], (rows, block))
                for tap in range(taps):
                    dist = (tap - (taps - 1)) if d == 0 else (taps - 1 - tap)
                    term = pad[SUB + dist : SUB + dist + rows, cols]
                    if dist != 0:
                        term = term * masks[dist]
                    total = total + cw_ref[d, tap : tap + 1, cols] * term
                u = (total / (1.0 + jnp.exp(-total))).astype(jnp.bfloat16)
                ubf[:, cols] = u
                u_ref[d, pl.ds(k, rows, stride=folds), :] = u.astype(jnp.float32)
            wcols = slice(cb * wide, (cb + 1) * wide)
            acc = acc + jnp.dot(
                ubf[:, wcols], xp_ref[d, wcols, :], preferred_element_type=jnp.float32
            )
        proj_ref[d * rows : (d + 1) * rows, :] = acc
        low = acc[:, :rank].astype(jnp.bfloat16)
        for cb in range(width // wide):
            wcols = slice(cb * wide, (cb + 1) * wide)
            v = jnp.dot(low, dp_ref[d, :, wcols], preferred_element_type=jnp.float32)
            v = v + db_ref[d : d + 1, wcols]
            step = jnp.maximum(v, 0.0) + jnp.log1p(jnp.exp(-jnp.abs(v)))
            for half in range(2):
                dt_ref[d, pl.ds(2 * cb + half, rows, stride=folds), :] = step[
                    :, half * LANES : (half + 1) * LANES
                ]
    copy = pltpu.make_async_copy(proj_ref, bc, sem)
    copy.start()
    copy.wait()


def sweep_one(d, states, rank, chunk, rows, folds, starts, base, rate_scr, skip_ref, dt_ref, u_ref, bc, y_ref, keep_last, parts_of=None):
    chunks = rows // chunk
    zero = jnp.zeros((SUB, LANES), jnp.float32)
    if True:
        for j in range(folds // SUB) if parts_of is None else parts_of:
            rates = [
                rate_scr[(d * states + n) * folds + j * SUB : (d * states + n) * folds + (j + 1) * SUB, :]
                for n in range(states)
            ]
            skip = skip_ref[d, j * SUB : (j + 1) * SUB, :]

            def chunk_step(ci, carry):
                hs, sdt = carry
                c = ci if d == 0 else chunks - 1 - ci
                keep = keep_at(starts, base + (c if d == 0 else c + 1) * chunk)
                hs = tuple(h * keep for h in hs)

                def row_step(i, inner_carry):
                    hs, sdt = inner_carry
                    t = c * chunk + (i if d == 0 else chunk - 1 - i)
                    spot = pl.ds(pl.multiple_of(t * folds + j * SUB, SUB), SUB)
                    dt = dt_ref[d, spot, :]
                    u = u_ref[d, spot, :]
                    dtu = dt * u
                    parts = [skip * u, None, None, None]
                    out = []
                    for n in range(states):
                        h = jnp.exp2(dt * rates[n]) * hs[n] + dtu * bc[d * rows + t, rank + n]
                        out.append(h)
                        term = h * bc[d * rows + t, rank + states + n]
                        q = n % 4
                        parts[q] = term if parts[q] is None else parts[q] + term
                    y = (parts[0] + parts[1]) + (parts[2] + parts[3])
                    if d == 0:
                        y_ref[spot, :] = y
                    else:
                        y_ref[spot, :] += y
                    return (tuple(out), sdt + dt)

                return lax.fori_loop(0, chunk, row_step, (hs, sdt), unroll=2)

            hs, sdt = lax.fori_loop(0, chunks, chunk_step, ((zero,) * states, zero))
            keep_last(j, hs, sdt)


def sweep_kernel(
    states, rank, chunk,
    me_ref, len_ref, inner_ref, prev_ref, next_ref, cw_ref, cb_ref, xp_ref, dp_ref, db_ref,
    decay_ref, skip_ref,
    dt_ref, proj_ref, y_ref, pay_ref,
    pad, u_ref, rate_scr, ubf, held, bc, sem,
):
    rows, width = inner_ref.shape
    folds = width // LANES
    starts = slide_starts(len_ref)
    base = me_ref[0] * rows
    spread_rates(decay_ref, rate_scr, folds)
    prepare(
        rank, starts, base, inner_ref, prev_ref, next_ref, cw_ref, cb_ref, xp_ref, dp_ref, db_ref,
        dt_ref, proj_ref, pad, u_ref, ubf, bc, sem,
    )
    for d in range(2):

        def keep_last(j, hs, sdt):
            for n in range(states):
                held[d * states + n, j * SUB : (j + 1) * SUB, :] = hs[n]
                held[d * states + n, folds + j * SUB : folds + (j + 1) * SUB, :] = sdt

        sweep_one(
            d, states, rank, chunk, rows, folds, starts, base, rate_scr, skip_ref, dt_ref, u_ref,
            bc, y_ref, keep_last,
        )
    pay_ref[...] = held[...].astype(jnp.bfloat16)


def relay_kernel(states, split, rows, chunk, me_ref, len_ref, got_ref, rate_ref, out_ref):
    shards = got_ref.shape[0]
    depth = got_ref.shape[1] // 2
    starts = slide_starts(len_ref)
    backward = me_ref[0] // split >= states
    rate = rate_ref[...] * -LOG2E

    def step(i, h):
        s = jnp.where(backward, shards - 1 - i, i)
        keep = jnp.float32(1.0)
        for c in range(rows // chunk):
            keep = keep * keep_at(
                starts, s * rows + c * chunk + jnp.where(backward, chunk, 0)
            )
        out_ref[s] = h.astype(jnp.bfloat16)
        got = got_ref[s].astype(jnp.float32)
        return jnp.exp2(rate * got[depth:]) * (h * keep) + got[:depth]

    lax.fori_loop(0, shards, step, jnp.zeros((depth, LANES), jnp.float32))


def finish_one(d, j, states, rank, chunk, rows, folds, starts, base, rate_scr, enter_of, dt_ref, bc, y_ref, tot):
    chunks = rows // chunk
    rates = [
        rate_scr[(d * states + n) * folds + j * SUB : (d * states + n) * folds + (j + 1) * SUB, :]
        for n in range(states)
    ]
    enters = [
        enter_of(n)
        for n in range(states)
    ]

    def chunk_step(ci, carry):
        alive, sdt = carry
        c = ci if d == 0 else chunks - 1 - ci
        alive = alive * keep_at(starts, base + (c if d == 0 else c + 1) * chunk)

        def row_step(i, sdt):
            t = c * chunk + (i if d == 0 else chunk - 1 - i)
            spot = pl.ds(pl.multiple_of(t * folds + j * SUB, SUB), SUB)
            sdt = sdt + dt_ref[d, spot, :]
            parts = [None] * 4
            for n in range(states):
                term = jnp.exp2(sdt * rates[n]) * (
                    enters[n] * bc[d * rows + t, rank + states + n]
                )
                q = n % 4
                parts[q] = term if parts[q] is None else parts[q] + term
            y = ((parts[0] + parts[1]) + (parts[2] + parts[3])) * alive
            if d == 0:
                tot[spot, :] = y_ref[spot, :] + y
            else:
                tot[spot, :] += y
            return sdt

        return (alive, lax.fori_loop(0, chunk, row_step, sdt, unroll=2))

    lax.fori_loop(
        0, chunks, chunk_step, (jnp.float32(1.0), jnp.zeros((SUB, LANES), jnp.float32))
    )


def finish_kernel(
    states, rank, chunk,
    me_ref, len_ref, bc, dt_ref, y_ref, enter_ref, decay_ref, place_ref,
    out_ref,
    rate_scr, tot,
):
    rows = place_ref.shape[0]
    folds = decay_ref.shape[2] // LANES
    starts = slide_starts(len_ref)
    base = me_ref[0] * rows
    spread_rates(decay_ref, rate_scr, folds)
    for d in range(2):
        for j in range(folds // SUB):

            def enter_of(n):
                return enter_ref[d * states + n, j * SUB : (j + 1) * SUB, :].astype(jnp.float32)

            finish_one(
                d, j, states, rank, chunk, rows, folds, starts, base, rate_scr, enter_of, dt_ref,
                bc, y_ref, tot,
            )
    pick = place_ref[...]
    for k in range(folds):
        part = tot[pl.ds(k, rows, stride=folds), :].astype(jnp.bfloat16)
        tot[pl.ds(k, rows, stride=folds), :] = lax.dot_general(
            pick, part, (((0,), (0,)), ((), ())), preferred_element_type=jnp.float32
        )
    out_ref[...] = tot[...].astype(jnp.bfloat16)


def peer_id(peer):
    count = lax.axis_size("slide")
    return {"seq": lax.div(peer, count), "slide": lax.rem(peer, count)}


def greet_all(shards, me):
    barrier = pltpu.get_barrier_semaphore()

    def greet(i, _):
        pl.semaphore_signal(
            barrier, inc=1, device_id=peer_id(lax.rem(me + i, shards)),
            device_id_type=pl.DeviceIdType.MESH,
        )
        return 0

    lax.fori_loop(1, shards, greet, 0)


def await_all(shards):
    pl.semaphore_wait(pltpu.get_barrier_semaphore(), shards - 1)


def block_copy(src, dst, i, me, shards, send_sem, recv_sem):
    peer = lax.rem(me + i, shards)
    return pltpu.make_async_remote_copy(
        src_ref=src.at[peer], dst_ref=dst.at[me], send_sem=send_sem.at[i],
        recv_sem=recv_sem.at[i], device_id=peer_id(peer),
        device_id_type=pl.DeviceIdType.MESH,
    )


def block_landed(src, dst, i, me, shards, send_sem, recv_sem):
    peer = lax.rem(me + i, shards)
    origin = lax.rem(me + shards - i, shards)
    return pltpu.make_async_remote_copy(
        src_ref=src.at[peer], dst_ref=dst.at[origin], send_sem=send_sem.at[i],
        recv_sem=recv_sem.at[i], device_id=peer_id(peer),
        device_id_type=pl.DeviceIdType.MESH,
    )


def start_blocks(*args):
    src, dst, me, shards, send_sem, recv_sem = args

    def go(i, _):
        block_copy(src, dst, i, me, shards, send_sem, recv_sem).start()
        return 0

    lax.fori_loop(1, shards, go, 0)


def await_blocks(*args):
    src, dst, me, shards, send_sem, recv_sem = args

    def stop(i, _):
        block_landed(src, dst, i, me, shards, send_sem, recv_sem).wait()
        return 0

    lax.fori_loop(1, shards, stop, 0)


def layer_kernel(
    shards, states, rank, chunk, groups,
    len_ref, emb_ref, slots_ref, cw_ref, cb_ref, db_ref, skip_ref,
    wg_ref, wi_ref, xp_hbm, dp_hbm, decay_hbm,
    out_ref,
    scr, send, got, gslot, ordered, wg, wi, xp_ref, dp_ref, decay_ref,
    inner_ref, prev_ref, next_ref, gate_ref, place_ref, skip_scr,
    dt_ref, proj_ref, y_ref, pad, u_ref, rate_scr, ubf, held, bc, sem,
    stage, gotf, passes, pay0, pay1, got0, got1, ent0, ent1, land0, land1, enters0, enters1,
    turn, back0, back1, back2, home0, home1, home2, send_sem, recv_sem, halo_send, halo_recv,
    load_sem,
):
    rows, width = inner_ref.shape
    model = emb_ref.shape[1]
    folds = width // LANES
    mfolds = model // LANES
    wide = 2 * LANES
    edge = prev_ref.shape[0]
    per = folds // groups
    quads = shards // groups
    some = states // quads
    tall = some * per
    me = lax.axis_index(AXES)
    pays, gots, ents, lands = (pay0, pay1), (got0, got1), (ent0, ent1), (land0, land1)
    backs, homes = (back0, back1, back2), (home0, home1, home2)
    enters = (enters0, enters1)
    f32, bf16 = jnp.float32, jnp.bfloat16

    def route(src, dst, number):
        return (src, dst, me, shards, send_sem.at[number], recv_sem.at[number])

    greet_all(shards, me)
    pairs = ((wg_ref, wg), (decay_hbm, decay_ref), (wi_ref, wi), (xp_hbm, xp_ref), (dp_hbm, dp_ref))
    loads = [
        pltpu.make_async_copy(src, dst, load_sem.at[i]) for i, (src, dst) in enumerate(pairs)
    ]
    for load in loads:
        load.start()
    for k in range(mfolds):
        scr[pl.ds(k, rows, stride=mfolds), :] = emb_ref[:, k * LANES : (k + 1) * LANES].astype(f32)
    send[...] = scr[...].astype(bf16).reshape(send.shape)
    await_all(shards)
    start_blocks(*route(slots_ref, gslot, 7))
    start_blocks(*route(send, got, 8))
    got[me] = send[me]
    gslot[me] = slots_ref[me]
    starts = slide_starts(len_ref)
    base = me * rows
    for k in range(folds):
        for d in range(2):
            skip_scr[d, k : k + 1, :] = skip_ref[d : d + 1, k * LANES : (k + 1) * LANES]
    stage[...] = jnp.zeros(stage.shape, f32)
    passes[...] = jnp.zeros(passes.shape, f32)
    loads[0].wait()

    def gate_tile(cb, _):
        cols = pl.ds(pl.multiple_of(cb * wide, wide), wide)
        v = jnp.dot(emb_ref[...], wg[:, cols], preferred_element_type=f32)
        gate_ref[:, cols] = v / (1.0 + jnp.exp(-v))
        return 0

    lax.fori_loop(0, width // wide, gate_tile, 0)
    loads[1].wait()
    spread_rates(decay_ref, rate_scr, folds)
    for load in loads[2:]:
        load.wait()
    await_blocks(*route(slots_ref, gslot, 7))
    await_blocks(*route(send, got, 8))
    slot_row = jnp.sum(gslot[...], axis=0)
    place = (
        jnp.broadcast_to(slot_row, (rows, rows))
        == lax.broadcasted_iota(jnp.int32, (rows, rows), 0).astype(f32)
    ).astype(bf16)
    place_ref[...] = place
    scr[...] = got[...].astype(f32).reshape(scr.shape)
    for k in range(mfolds):
        ordered[:, k * LANES : (k + 1) * LANES] = jnp.dot(
            place, scr[pl.ds(k, rows, stride=mfolds), :].astype(bf16), preferred_element_type=f32
        ).astype(bf16)

    def inner_tile(cb, _):
        cols = pl.ds(pl.multiple_of(cb * wide, wide), wide)
        inner_ref[:, cols] = jnp.dot(
            ordered[...], wi[:, cols], preferred_element_type=f32
        ).astype(bf16)
        return 0

    lax.fori_loop(0, width // wide, inner_tile, 0)
    to_next = pltpu.make_async_remote_copy(
        src_ref=inner_ref.at[pl.ds(rows - edge, edge)], dst_ref=prev_ref,
        send_sem=halo_send.at[0], recv_sem=halo_recv.at[0],
        device_id=peer_id(lax.rem(me + 1, shards)), device_id_type=pl.DeviceIdType.MESH,
    )
    to_prev = pltpu.make_async_remote_copy(
        src_ref=inner_ref.at[pl.ds(0, edge)], dst_ref=next_ref,
        send_sem=halo_send.at[1], recv_sem=halo_recv.at[1],
        device_id=peer_id(lax.rem(me + shards - 1, shards)), device_id_type=pl.DeviceIdType.MESH,
    )
    to_next.start()
    to_prev.start()
    to_next.wait()
    to_prev.wait()
    prepare(
        rank, starts, base, inner_ref, prev_ref, next_ref, cw_ref, cb_ref, xp_ref, dp_ref, db_ref,
        dt_ref, proj_ref, pad, u_ref, ubf, bc, sem,
    )

    def keep_last(j, hs, sdt):
        for n in range(states):
            held[n * folds + j * SUB : n * folds + (j + 1) * SUB, :] = hs[n]
        held[states * folds + j * SUB : states * folds + (j + 1) * SUB, :] = sdt

    def sweep(d, parts_of):
        sweep_one(
            d, states, rank, chunk, rows, folds, starts, base, rate_scr, skip_scr, dt_ref, u_ref,
            bc, y_ref, keep_last, parts_of,
        )

    def pack(d):
        for g in range(groups):
            for q in range(quads):
                spot = (g * quads + q) * 2 * SUB
                for m in range(some):
                    row = (q * some + m) * folds + g * per
                    stage[spot + m * per : spot + (m + 1) * per, :] = held[row : row + per, :]
                row = states * folds + g * per
                stage[spot + tall : spot + tall + per, :] = held[row : row + per, :]
        pays[d][...] = stage[...].astype(bf16).reshape(pays[d].shape)

    def launch(d):
        start_blocks(*route(pays[d], gots[d], d))
        gots[d][me] = pays[d][me]

    def relay(d):
        await_blocks(*route(pays[d], gots[d], d))
        gotf[...] = gots[d][...].astype(f32)
        for m in range(some):
            row = (d * states + lax.rem(me, quads) * some + m) * folds + lax.div(me, quads) * per
            for f in range(per):
                rate = rate_scr[pl.ds(row + f, 1), :]
                passes[:, m * per + f : m * per + f + 1, :] = jnp.exp2(
                    rate[None] * gotf[:, tall + f : tall + f + 1, :]
                )

        def step(i, h):
            s = i if d == 0 else shards - 1 - i
            keep = jnp.float32(1.0)
            for c in range(rows // chunk):
                keep = keep * keep_at(starts, s * rows + c * chunk + d * chunk)
            ents[d][s] = h.astype(bf16)
            return passes[s] * (h * keep) + gotf[s]

        lax.fori_loop(0, shards, step, jnp.zeros((2 * SUB, LANES), f32))
        start_blocks(*route(ents[d], lands[d], 2 + d))
        lands[d][me] = ents[d][me]

    def arrive(d):
        await_blocks(*route(ents[d], lands[d], 2 + d))
        gotf[...] = lands[d][...].astype(f32)
        for g in range(groups):
            for q in range(quads):
                for m in range(some):
                    row = (q * some + m) * folds + g * per
                    enters[d][row : row + per, :] = gotf[g * quads + q, m * per : (m + 1) * per, :]

    def finish(d, j):
        def enter_of(n):
            return enters[d][n * folds + j * SUB : n * folds + (j + 1) * SUB, :]

        finish_one(
            d, j, states, rank, chunk, rows, folds, starts, base, rate_scr, enter_of, dt_ref, bc,
            y_ref, y_ref,
        )

    def give(j):
        for k in range(SUB):
            part = y_ref[pl.ds(j * SUB + k, rows, stride=folds), :].astype(bf16)
            turn[pl.ds(k, rows, stride=SUB), :] = lax.dot_general(
                place_ref[...], part, (((0,), (0,)), ((), ())), preferred_element_type=f32
            )
        backs[j][...] = turn[...].astype(bf16).reshape(backs[j].shape)
        start_blocks(*route(backs[j], homes[j], 4 + j))
        homes[j][me] = backs[j][me]

    sweep(0, (0, 1, 2))
    pack(0)
    launch(0)
    sweep(1, (0, 1))
    relay(0)
    sweep(1, (2,))
    pack(1)
    launch(1)
    arrive(0)
    finish(0, 0)
    relay(1)
    finish(0, 1)
    arrive(1)
    finish(1, 0)
    give(0)
    finish(1, 1)
    give(1)
    finish(0, 2)
    finish(1, 2)
    give(2)
    for j in range(folds // SUB):
        await_blocks(*route(backs[j], homes[j], 4 + j))
        turn[...] = homes[j][...].astype(f32).reshape(turn.shape)
        for k in range(SUB):
            cols = slice((j * SUB + k) * LANES, (j * SUB + k + 1) * LANES)
            out_ref[:, cols] = (
                turn[pl.ds(k, rows, stride=SUB), :] * gate_ref[:, cols]
            ).astype(bf16)


def local(
    tile_embed, destination, slide_lengths, w_inner, w_gate, conv_weight, conv_bias, x_project,
    dt_project, dt_bias, decay, skip_gain,
):
    shards = lax.axis_size(AXES)
    rows, model = tile_embed.shape
    width = w_inner.shape[1]
    states = decay.shape[1]
    rank = dt_project.shape[1]
    taps = conv_weight.shape[1]
    folds = width // LANES
    per_peer = rows // shards
    chunk = min(shards, rows)
    split = shards // (2 * states)
    halo = taps - 1
    me = lax.axis_index(AXES).astype(jnp.int32)
    me_arr = me[None]
    f32, bf16 = jnp.float32, jnp.bfloat16
    vmem = pl.BlockSpec(memory_space=pltpu.VMEM)
    smem = pl.BlockSpec(memory_space=pltpu.SMEM)
    params = pltpu.CompilerParams(vmem_limit_bytes=60 * 1024 * 1024)

    any_space = pl.BlockSpec(memory_space=pl.ANY)
    mfolds = model // LANES
    groups = 8
    fast = (
        shards == 2 * states and shards % groups == 0 and folds == 3 * SUB
        and states % (shards // groups) == 0 and (per_peer * mfolds) % 16 == 0
        and (per_peer * SUB) % 16 == 0
    )

    def remote_params(number):
        return pltpu.CompilerParams(
            vmem_limit_bytes=60 * 1024 * 1024, collective_id=number, has_side_effects=True
        )

    if fast:
        lane = jnp.arange(rows, dtype=jnp.int32)[None, :]
        slots = jnp.tile((destination % rows).astype(f32).reshape(shards, per_peer), (1, shards))
        slots = jnp.where(lane // per_peer == me, slots, 0.0)[:, None, :]
        sent_rows = pltpu.VMEM((shards, per_peer * mfolds, LANES), bf16)
        cell = pltpu.VMEM((shards, 2 * SUB, LANES), bf16)
        third = pltpu.VMEM((shards, per_peer * SUB, LANES), bf16)
        return pl.pallas_call(
            functools.partial(layer_kernel, shards, states, rank, chunk, groups),
            out_shape=jax.ShapeDtypeStruct((rows, width), bf16),
            in_specs=[smem] + [vmem] * 6 + [any_space] * 5,
            out_specs=vmem,
            scratch_shapes=[
                pltpu.VMEM((rows * mfolds, LANES), f32),
                sent_rows, sent_rows,
                pltpu.VMEM((shards, 1, rows), f32),
                pltpu.VMEM((rows, model), bf16),
                pltpu.VMEM((model, width), bf16),
                pltpu.VMEM((model, width), bf16),
                pltpu.VMEM(x_project.shape, bf16),
                pltpu.VMEM(dt_project.shape, bf16),
                pltpu.VMEM(decay.shape, f32),
                pltpu.VMEM((rows, width), bf16),
                pltpu.VMEM((2 * SUB, width), bf16),
                pltpu.VMEM((2 * SUB, width), bf16),
                pltpu.VMEM((rows, width), f32),
                pltpu.VMEM((rows, rows), bf16),
                pltpu.VMEM((2, folds, LANES), f32),
                pltpu.VMEM((2, rows * folds, LANES), f32),
                pltpu.VMEM((2 * rows, LANES), f32),
                pltpu.VMEM((rows * folds, LANES), f32),
                pltpu.VMEM((rows + 2 * SUB, width), f32),
                pltpu.VMEM((2, rows * folds, LANES), f32),
                pltpu.VMEM((2 * states * folds, LANES), f32),
                pltpu.VMEM((rows, width), bf16),
                pltpu.VMEM(((states + 1) * folds, LANES), f32),
                pltpu.SMEM((2 * rows, LANES), f32),
                pltpu.SemaphoreType.DMA,
                pltpu.VMEM((shards * 2 * SUB, LANES), f32),
                pltpu.VMEM((shards, 2 * SUB, LANES), f32),
                pltpu.VMEM((shards, 2 * SUB, LANES), f32),
                cell, cell, cell, cell, cell, cell, cell, cell,
                pltpu.VMEM((states * folds, LANES), f32),
                pltpu.VMEM((states * folds, LANES), f32),
                pltpu.VMEM((rows * SUB, LANES), f32),
                third, third, third, third, third, third,
                pltpu.SemaphoreType.DMA((9, shards)),
                pltpu.SemaphoreType.DMA((9, shards)),
                pltpu.SemaphoreType.DMA((2,)),
                pltpu.SemaphoreType.DMA((2,)),
                pltpu.SemaphoreType.DMA((5,)),
            ],
            compiler_params=remote_params(2),
            name="layer",
        )(
            slide_lengths, tile_embed, slots, conv_weight, conv_bias, dt_bias, skip_gain,
            w_gate, w_inner, x_project, dt_project, decay,
        )
    slot_col = jnp.broadcast_to((destination % rows).astype(bf16)[:, None], (rows, LANES))
    sent = jnp.concatenate([tile_embed, slot_col], axis=1).reshape(shards, per_peer, model + LANES)
    got = lax.all_to_all(sent, AXES, split_axis=0, concat_axis=0, tiled=True)
    got = got.reshape(rows, model + LANES)
    slot = got[:, model].astype(jnp.int32)
    place = (slot[None, :] == jnp.arange(rows, dtype=jnp.int32)[:, None]).astype(bf16)
    ordered = jnp.dot(place, got[:, :model], preferred_element_type=f32).astype(bf16)
    inner = jnp.dot(ordered, w_inner, preferred_element_type=f32).astype(bf16)
    up = [(i, i + 1) for i in range(shards - 1)]
    down = [(i + 1, i) for i in range(shards - 1)]
    before = lax.ppermute(inner[rows - 2 * SUB :], AXES, up)
    after = lax.ppermute(inner[: 2 * SUB], AXES, down)
    dt, proj, y, pay = pl.pallas_call(
        functools.partial(sweep_kernel, states, rank, chunk),
        out_shape=(
            jax.ShapeDtypeStruct((2, rows * folds, LANES), f32),
            jax.ShapeDtypeStruct((2 * rows, LANES), f32),
            jax.ShapeDtypeStruct((rows * folds, LANES), f32),
            jax.ShapeDtypeStruct((2 * states, 2 * folds, LANES), bf16),
        ),
        in_specs=[smem, smem] + [vmem] * 10,
        out_specs=(vmem,) * 4,
        scratch_shapes=[
            pltpu.VMEM((rows + 2 * SUB, width), f32),
            pltpu.VMEM((2, rows * folds, LANES), f32),
            pltpu.VMEM((2 * states * folds, LANES), f32),
            pltpu.VMEM((rows, width), bf16),
            pltpu.VMEM((2 * states, 2 * folds, LANES), f32),
            pltpu.SMEM((2 * rows, LANES), f32),
            pltpu.SemaphoreType.DMA,
        ],
        compiler_params=params,
        name="sweep",
    )(
        me_arr, slide_lengths, inner, before, after, conv_weight, conv_bias,
        x_project, dt_project, dt_bias, decay,
        skip_gain.reshape(2, folds, LANES),
    )
    pay = pay.reshape(2 * states, 2, split, folds // split, LANES)
    pay = pay.swapaxes(1, 2).reshape(shards, 2 * folds // split, LANES)
    theirs = lax.all_to_all(pay, AXES, split_axis=0, concat_axis=0, tiled=True)
    my_rate = lax.dynamic_slice_in_dim(
        decay.reshape(shards, folds // split, LANES), me, 1, axis=0
    )[0]
    enter = pl.pallas_call(
        functools.partial(relay_kernel, states, split, rows, chunk),
        out_shape=jax.ShapeDtypeStruct((shards, folds // split, LANES), bf16),
        in_specs=[smem, smem, vmem, vmem],
        out_specs=vmem,
        compiler_params=params,
        name="relay",
    )(me_arr, slide_lengths, theirs, my_rate)
    enter = lax.all_to_all(enter, AXES, split_axis=0, concat_axis=0, tiled=True)
    enter = enter.reshape(2 * states, folds, LANES)
    back = pl.pallas_call(
        functools.partial(finish_kernel, states, rank, chunk),
        out_shape=jax.ShapeDtypeStruct((rows * folds, LANES), bf16),
        in_specs=[smem, smem, smem] + [vmem] * 5,
        out_specs=vmem,
        scratch_shapes=[
            pltpu.VMEM((2 * states * folds, LANES), f32),
            pltpu.VMEM((rows * folds, LANES), f32),
        ],
        compiler_params=params,
        name="finish",
    )(
        me_arr, slide_lengths, proj, dt, y, enter, decay,
        place,
    )
    back = back.reshape(shards, per_peer, width)
    returned = lax.all_to_all(back, AXES, split_axis=0, concat_axis=0, tiled=True)
    gate = jnp.dot(tile_embed, w_gate, preferred_element_type=f32)
    return (returned.reshape(rows, width).astype(f32) * jax.nn.silu(gate)).astype(bf16)


def solution(mesh):
    placed = (P(AXES, None), P(AXES)) + (P(),) * 10
    return jax.shard_map(
        local, mesh=mesh, in_specs=placed, out_specs=P(AXES, None), check_vma=False
    )
```

```python
import functools

import jax
import jax.numpy as jnp
from jax import lax
from jax.experimental import pallas as pl
from jax.experimental.pallas import tpu as pltpu
from jax.sharding import PartitionSpec as P

AXES = ("seq", "slide")
LANES = 128
SUB = 8
LOG2E = 1.4426950408889634


def slide_starts(len_ref):
    starts = [jnp.int32(0)]
    for s in range(len_ref.shape[0]):
        starts.append(starts[-1] + len_ref[s])
    return starts


def keep_at(starts, pos):
    hit = pos == starts[0]
    for s in starts[1:]:
        hit = jnp.logical_or(hit, pos == s)
    return jnp.where(hit, 0.0, 1.0).astype(jnp.float32)


def spread_rates(decay_ref, rate_scr, folds):
    count = decay_ref.shape[1]
    for d in range(2):
        for k in range(folds):
            rate_scr[pl.ds(d * count * folds + k, count, stride=folds), :] = (
                decay_ref[d, :, k * LANES : (k + 1) * LANES] * -LOG2E
            )


def prepare(
    rank, starts, base, inner_ref, prev_ref, next_ref, cw_ref, cb_ref, xp_ref, dp_ref, db_ref,
    dt_ref, proj_ref, pad, u_ref, ubf, bc, sem,
):
    rows, width = inner_ref.shape
    folds = width // LANES
    taps = cw_ref.shape[1]
    halo = prev_ref.shape[0]
    pad[0:SUB, :] = prev_ref[halo - SUB :, :].astype(jnp.float32)
    pad[SUB : SUB + rows, :] = inner_ref[...].astype(jnp.float32)
    pad[SUB + rows : 2 * SUB + rows, :] = next_ref[0:SUB, :].astype(jnp.float32)
    where_at = base + lax.broadcasted_iota(jnp.int32, (rows, LANES), 0)
    masks = {}
    for dist in range(1, taps):
        for sign in (-1, 1):
            bad = jnp.zeros((rows, LANES), jnp.bool_)
            for s in starts:
                if sign < 0:
                    bad = bad | ((where_at - dist < s) & (where_at >= s))
                else:
                    bad = bad | ((where_at < s) & (where_at + dist >= s))
            masks[sign * dist] = jnp.where(bad, 0.0, 1.0)
    block = LANES
    wide = 2 * LANES
    for d in range(2):
        acc = jnp.zeros((rows, LANES), jnp.float32)
        for cb in range(width // wide):
            for half in range(2):
                k = 2 * cb + half
                cols = slice(k * block, (k + 1) * block)
                total = jnp.broadcast_to(cb_ref[d : d + 1, cols], (rows, block))
                for tap in range(taps):
                    dist = (tap - (taps - 1)) if d == 0 else (taps - 1 - tap)
                    term = pad[SUB + dist : SUB + dist + rows, cols]
                    if dist != 0:
                        term = term * masks[dist]
                    total = total + cw_ref[d, tap : tap + 1, cols] * term
                u = (total / (1.0 + jnp.exp(-total))).astype(jnp.bfloat16)
                ubf[:, cols] = u
                u_ref[d, pl.ds(k, rows, stride=folds), :] = u.astype(jnp.float32)
            wcols = slice(cb * wide, (cb + 1) * wide)
            acc = acc + jnp.dot(
                ubf[:, wcols], xp_ref[d, wcols, :], preferred_element_type=jnp.float32
            )
        proj_ref[d * rows : (d + 1) * rows, :] = acc
        low = acc[:, :rank].astype(jnp.bfloat16)
        for cb in range(width // wide):
            wcols = slice(cb * wide, (cb + 1) * wide)
            v = jnp.dot(low, dp_ref[d, :, wcols], preferred_element_type=jnp.float32)
            v = v + db_ref[d : d + 1, wcols]
            step = jnp.maximum(v, 0.0) + jnp.log1p(jnp.exp(-jnp.abs(v)))
            for half in range(2):
                dt_ref[d, pl.ds(2 * cb + half, rows, stride=folds), :] = step[
                    :, half * LANES : (half + 1) * LANES
                ]
    copy = pltpu.make_async_copy(proj_ref, bc, sem)
    copy.start()
    copy.wait()


def sweep_one(d, states, rank, chunk, rows, folds, starts, base, rate_scr, skip_ref, dt_ref, u_ref, bc, y_ref, keep_last, parts_of=None):
    chunks = rows // chunk
    zero = jnp.zeros((SUB, LANES), jnp.float32)
    if True:
        for j in range(folds // SUB) if parts_of is None else parts_of:
            rates = [
                rate_scr[(d * states + n) * folds + j * SUB : (d * states + n) * folds + (j + 1) * SUB, :]
                for n in range(states)
            ]
            skip = skip_ref[d, j * SUB : (j + 1) * SUB, :]

            def chunk_step(ci, carry):
                hs, sdt = carry
                c = ci if d == 0 else chunks - 1 - ci
                keep = keep_at(starts, base + (c if d == 0 else c + 1) * chunk)
                hs = tuple(h * keep for h in hs)

                def row_step(i, inner_carry):
                    hs, sdt = inner_carry
                    t = c * chunk + (i if d == 0 else chunk - 1 - i)
                    spot = pl.ds(pl.multiple_of(t * folds + j * SUB, SUB), SUB)
                    dt = dt_ref[d, spot, :]
                    u = u_ref[d, spot, :]
                    dtu = dt * u
                    parts = [skip * u, None, None, None]
                    out = []
                    for n in range(states):
                        h = jnp.exp2(dt * rates[n]) * hs[n] + dtu * bc[d * rows + t, rank + n]
                        out.append(h)
                        term = h * bc[d * rows + t, rank + states + n]
                        q = n % 4
                        parts[q] = term if parts[q] is None else parts[q] + term
                    y = (parts[0] + parts[1]) + (parts[2] + parts[3])
                    if d == 0:
                        y_ref[spot, :] = y
                    else:
                        y_ref[spot, :] += y
                    return (tuple(out), sdt + dt)

                return lax.fori_loop(0, chunk, row_step, (hs, sdt), unroll=8)

            hs, sdt = lax.fori_loop(0, chunks, chunk_step, ((zero,) * states, zero))
            keep_last(j, hs, sdt)


def sweep_kernel(
    states, rank, chunk,
    me_ref, len_ref, inner_ref, prev_ref, next_ref, cw_ref, cb_ref, xp_ref, dp_ref, db_ref,
    decay_ref, skip_ref,
    dt_ref, proj_ref, y_ref, pay_ref,
    pad, u_ref, rate_scr, ubf, held, bc, sem,
):
    rows, width = inner_ref.shape
    folds = width // LANES
    starts = slide_starts(len_ref)
    base = me_ref[0] * rows
    spread_rates(decay_ref, rate_scr, folds)
    prepare(
        rank, starts, base, inner_ref, prev_ref, next_ref, cw_ref, cb_ref, xp_ref, dp_ref, db_ref,
        dt_ref, proj_ref, pad, u_ref, ubf, bc, sem,
    )
    for d in range(2):

        def keep_last(j, hs, sdt):
            for n in range(states):
                held[d * states + n, j * SUB : (j + 1) * SUB, :] = hs[n]
                held[d * states + n, folds + j * SUB : folds + (j + 1) * SUB, :] = sdt

        sweep_one(
            d, states, rank, chunk, rows, folds, starts, base, rate_scr, skip_ref, dt_ref, u_ref,
            bc, y_ref, keep_last,
        )
    pay_ref[...] = held[...].astype(jnp.bfloat16)


def relay_kernel(states, split, rows, chunk, me_ref, len_ref, got_ref, rate_ref, out_ref):
    shards = got_ref.shape[0]
    depth = got_ref.shape[1] // 2
    starts = slide_starts(len_ref)
    backward = me_ref[0] // split >= states
    rate = rate_ref[...] * -LOG2E

    def step(i, h):
        s = jnp.where(backward, shards - 1 - i, i)
        keep = jnp.float32(1.0)
        for c in range(rows // chunk):
            keep = keep * keep_at(
                starts, s * rows + c * chunk + jnp.where(backward, chunk, 0)
            )
        out_ref[s] = h.astype(jnp.bfloat16)
        got = got_ref[s].astype(jnp.float32)
        return jnp.exp2(rate * got[depth:]) * (h * keep) + got[:depth]

    lax.fori_loop(0, shards, step, jnp.zeros((depth, LANES), jnp.float32))


def finish_one(d, j, states, rank, chunk, rows, folds, starts, base, rate_scr, enter_of, dt_ref, bc, y_ref, tot):
    chunks = rows // chunk
    rates = [
        rate_scr[(d * states + n) * folds + j * SUB : (d * states + n) * folds + (j + 1) * SUB, :]
        for n in range(states)
    ]
    enters = [
        enter_of(n)
        for n in range(states)
    ]

    def chunk_step(ci, carry):
        alive, sdt = carry
        c = ci if d == 0 else chunks - 1 - ci
        alive = alive * keep_at(starts, base + (c if d == 0 else c + 1) * chunk)

        def row_step(i, sdt):
            t = c * chunk + (i if d == 0 else chunk - 1 - i)
            spot = pl.ds(pl.multiple_of(t * folds + j * SUB, SUB), SUB)
            sdt = sdt + dt_ref[d, spot, :]
            parts = [None] * 4
            for n in range(states):
                term = jnp.exp2(sdt * rates[n]) * (
                    enters[n] * bc[d * rows + t, rank + states + n]
                )
                q = n % 4
                parts[q] = term if parts[q] is None else parts[q] + term
            y = ((parts[0] + parts[1]) + (parts[2] + parts[3])) * alive
            if d == 0:
                tot[spot, :] = y_ref[spot, :] + y
            else:
                tot[spot, :] += y
            return sdt

        return (alive, lax.fori_loop(0, chunk, row_step, sdt, unroll=8))

    lax.fori_loop(
        0, chunks, chunk_step, (jnp.float32(1.0), jnp.zeros((SUB, LANES), jnp.float32))
    )


def finish_kernel(
    states, rank, chunk,
    me_ref, len_ref, bc, dt_ref, y_ref, enter_ref, decay_ref, place_ref,
    out_ref,
    rate_scr, tot,
):
    rows = place_ref.shape[0]
    folds = decay_ref.shape[2] // LANES
    starts = slide_starts(len_ref)
    base = me_ref[0] * rows
    spread_rates(decay_ref, rate_scr, folds)
    for d in range(2):
        for j in range(folds // SUB):

            def enter_of(n):
                return enter_ref[d * states + n, j * SUB : (j + 1) * SUB, :].astype(jnp.float32)

            finish_one(
                d, j, states, rank, chunk, rows, folds, starts, base, rate_scr, enter_of, dt_ref,
                bc, y_ref, tot,
            )
    pick = place_ref[...]
    for k in range(folds):
        part = tot[pl.ds(k, rows, stride=folds), :].astype(jnp.bfloat16)
        tot[pl.ds(k, rows, stride=folds), :] = lax.dot_general(
            pick, part, (((0,), (0,)), ((), ())), preferred_element_type=jnp.float32
        )
    out_ref[...] = tot[...].astype(jnp.bfloat16)


def peer_id(peer):
    count = lax.axis_size("slide")
    return {"seq": lax.div(peer, count), "slide": lax.rem(peer, count)}


def greet_all(shards, me):
    barrier = pltpu.get_barrier_semaphore()

    def greet(i, _):
        pl.semaphore_signal(
            barrier, inc=1, device_id=peer_id(lax.rem(me + i, shards)),
            device_id_type=pl.DeviceIdType.MESH,
        )
        return 0

    lax.fori_loop(1, shards, greet, 0)


def await_all(shards):
    pl.semaphore_wait(pltpu.get_barrier_semaphore(), shards - 1)


def start_blocks(src, dst, me, shards, send_sem, recv_sem):
    def go(i, _):
        peer = lax.rem(me + i, shards)
        pltpu.make_async_remote_copy(
            src_ref=src.at[peer], dst_ref=dst.at[me], send_sem=send_sem, recv_sem=recv_sem,
            device_id=peer_id(peer), device_id_type=pl.DeviceIdType.MESH,
        ).start()
        return 0

    lax.fori_loop(1, shards, go, 0)


def await_blocks(src, dst, me, shards, send_sem, recv_sem):
    others = pl.ds(0, shards - 1)
    pltpu.make_async_remote_copy(
        src_ref=src.at[others], dst_ref=dst.at[others], send_sem=send_sem, recv_sem=recv_sem,
        device_id=peer_id(lax.rem(me + 1, shards)), device_id_type=pl.DeviceIdType.MESH,
    ).wait()


def layer_kernel(
    shards, states, rank, chunk, groups,
    len_ref, emb_ref, slots_ref, cw_ref, cb_ref, db_ref, skip_ref,
    wg_ref, wi_ref, xp_hbm, dp_hbm, decay_hbm,
    out_ref,
    scr, send, got, gslot, ordered, wg, wi, xp_ref, dp_ref, decay_ref,
    inner_ref, prev_ref, next_ref, gate_ref, place_ref, skip_scr,
    dt_ref, proj_ref, y_ref, pad, u_ref, rate_scr, ubf, held, bc, sem,
    stage, gotf, passes, pay0, pay1, got0, got1, ent0, ent1, land0, land1, enters0, enters1,
    turn, back0, back1, back2, home0, home1, home2, send_sem, recv_sem, halo_send, halo_recv,
    load_sem,
):
    rows, width = inner_ref.shape
    model = emb_ref.shape[1]
    folds = width // LANES
    mfolds = model // LANES
    wide = 2 * LANES
    edge = prev_ref.shape[0]
    per = folds // groups
    quads = shards // groups
    some = states // quads
    tall = some * per
    me = lax.axis_index(AXES)
    pays, gots, ents, lands = (pay0, pay1), (got0, got1), (ent0, ent1), (land0, land1)
    backs, homes = (back0, back1, back2), (home0, home1, home2)
    enters = (enters0, enters1)
    f32, bf16 = jnp.float32, jnp.bfloat16

    def route(src, dst, number):
        return (src, dst, me, shards, send_sem.at[number], recv_sem.at[number])

    greet_all(shards, me)
    pairs = ((wg_ref, wg), (decay_hbm, decay_ref), (wi_ref, wi), (xp_hbm, xp_ref), (dp_hbm, dp_ref))
    loads = [
        pltpu.make_async_copy(src, dst, load_sem.at[i]) for i, (src, dst) in enumerate(pairs)
    ]
    for load in loads:
        load.start()
    for k in range(mfolds):
        scr[pl.ds(k, rows, stride=mfolds), :] = emb_ref[:, k * LANES : (k + 1) * LANES].astype(f32)
    send[...] = scr[...].astype(bf16).reshape(send.shape)
    await_all(shards)
    start_blocks(*route(slots_ref, gslot, 7))
    start_blocks(*route(send, got, 8))
    got[me] = send[me]
    gslot[me] = slots_ref[me]
    starts = slide_starts(len_ref)
    base = me * rows
    for k in range(folds):
        for d in range(2):
            skip_scr[d, k : k + 1, :] = skip_ref[d : d + 1, k * LANES : (k + 1) * LANES]
    stage[...] = jnp.zeros(stage.shape, f32)
    passes[...] = jnp.zeros(passes.shape, f32)
    loads[0].wait()

    def gate_tile(cb, _):
        cols = pl.ds(pl.multiple_of(cb * wide, wide), wide)
        v = jnp.dot(emb_ref[...], wg[:, cols], preferred_element_type=f32)
        gate_ref[:, cols] = v / (1.0 + jnp.exp(-v))
        return 0

    lax.fori_loop(0, width // wide, gate_tile, 0)
    loads[1].wait()
    spread_rates(decay_ref, rate_scr, folds)
    for load in loads[2:]:
        load.wait()
    await_blocks(*route(slots_ref, gslot, 7))
    await_blocks(*route(send, got, 8))
    slot_row = jnp.sum(gslot[...], axis=0)
    place = (
        jnp.broadcast_to(slot_row, (rows, rows))
        == lax.broadcasted_iota(jnp.int32, (rows, rows), 0).astype(f32)
    ).astype(bf16)
    place_ref[...] = place
    scr[...] = got[...].astype(f32).reshape(scr.shape)
    for k in range(mfolds):
        ordered[:, k * LANES : (k + 1) * LANES] = jnp.dot(
            place, scr[pl.ds(k, rows, stride=mfolds), :].astype(bf16), preferred_element_type=f32
        ).astype(bf16)

    def inner_tile(cb, _):
        cols = pl.ds(pl.multiple_of(cb * wide, wide), wide)
        inner_ref[:, cols] = jnp.dot(
            ordered[...], wi[:, cols], preferred_element_type=f32
        ).astype(bf16)
        return 0

    lax.fori_loop(0, width // wide, inner_tile, 0)
    to_next = pltpu.make_async_remote_copy(
        src_ref=inner_ref.at[pl.ds(rows - edge, edge)], dst_ref=prev_ref,
        send_sem=halo_send.at[0], recv_sem=halo_recv.at[0],
        device_id=peer_id(lax.rem(me + 1, shards)), device_id_type=pl.DeviceIdType.MESH,
    )
    to_prev = pltpu.make_async_remote_copy(
        src_ref=inner_ref.at[pl.ds(0, edge)], dst_ref=next_ref,
        send_sem=halo_send.at[1], recv_sem=halo_recv.at[1],
        device_id=peer_id(lax.rem(me + shards - 1, shards)), device_id_type=pl.DeviceIdType.MESH,
    )
    to_next.start()
    to_prev.start()
    to_next.wait()
    to_prev.wait()
    prepare(
        rank, starts, base, inner_ref, prev_ref, next_ref, cw_ref, cb_ref, xp_ref, dp_ref, db_ref,
        dt_ref, proj_ref, pad, u_ref, ubf, bc, sem,
    )

    def keep_last(j, hs, sdt):
        for n in range(states):
            held[n * folds + j * SUB : n * folds + (j + 1) * SUB, :] = hs[n]
        held[states * folds + j * SUB : states * folds + (j + 1) * SUB, :] = sdt

    def sweep(d, parts_of):
        sweep_one(
            d, states, rank, chunk, rows, folds, starts, base, rate_scr, skip_scr, dt_ref, u_ref,
            bc, y_ref, keep_last, parts_of,
        )

    def pack(d):
        for g in range(groups):
            for q in range(quads):
                spot = (g * quads + q) * 2 * SUB
                for m in range(some):
                    row = (q * some + m) * folds + g * per
                    stage[spot + m * per : spot + (m + 1) * per, :] = held[row : row + per, :]
                row = states * folds + g * per
                stage[spot + tall : spot + tall + per, :] = held[row : row + per, :]
        pays[d][...] = stage[...].astype(bf16).reshape(pays[d].shape)

    def launch(d):
        start_blocks(*route(pays[d], gots[d], d))
        gots[d][me] = pays[d][me]

    def relay(d):
        await_blocks(*route(pays[d], gots[d], d))
        gotf[...] = gots[d][...].astype(f32)
        for m in range(some):
            row = (d * states + lax.rem(me, quads) * some + m) * folds + lax.div(me, quads) * per
            for f in range(per):
                rate = rate_scr[pl.ds(row + f, 1), :]
                passes[:, m * per + f : m * per + f + 1, :] = jnp.exp2(
                    rate[None] * gotf[:, tall + f : tall + f + 1, :]
                )

        def step(i, h):
            s = i if d == 0 else shards - 1 - i
            keep = jnp.float32(1.0)
            for c in range(rows // chunk):
                keep = keep * keep_at(starts, s * rows + c * chunk + d * chunk)
            ents[d][s] = h.astype(bf16)
            return passes[s] * (h * keep) + gotf[s]

        lax.fori_loop(0, shards, step, jnp.zeros((2 * SUB, LANES), f32), unroll=4)
        start_blocks(*route(ents[d], lands[d], 2 + d))
        lands[d][me] = ents[d][me]

    def arrive(d):
        await_blocks(*route(ents[d], lands[d], 2 + d))
        gotf[...] = lands[d][...].astype(f32)
        for g in range(groups):
            for q in range(quads):
                for m in range(some):
                    row = (q * some + m) * folds + g * per
                    enters[d][row : row + per, :] = gotf[g * quads + q, m * per : (m + 1) * per, :]

    def finish(d, j):
        def enter_of(n):
            return enters[d][n * folds + j * SUB : n * folds + (j + 1) * SUB, :]

        finish_one(
            d, j, states, rank, chunk, rows, folds, starts, base, rate_scr, enter_of, dt_ref, bc,
            y_ref, y_ref,
        )

    def give(j):
        for k in range(SUB):
            part = y_ref[pl.ds(j * SUB + k, rows, stride=folds), :].astype(bf16)
            turn[pl.ds(k, rows, stride=SUB), :] = lax.dot_general(
                place_ref[...], part, (((0,), (0,)), ((), ())), preferred_element_type=f32
            )
        backs[j][...] = turn[...].astype(bf16).reshape(backs[j].shape)
        start_blocks(*route(backs[j], homes[j], 4 + j))
        homes[j][me] = backs[j][me]

    sweep(0, (0, 1, 2))
    pack(0)
    launch(0)
    sweep(1, (0, 1))
    relay(0)
    sweep(1, (2,))
    pack(1)
    launch(1)
    arrive(0)
    finish(0, 0)
    relay(1)
    finish(0, 1)
    arrive(1)
    finish(1, 0)
    give(0)
    finish(1, 1)
    give(1)
    finish(0, 2)
    finish(1, 2)
    give(2)
    for j in range(folds // SUB):
        await_blocks(*route(backs[j], homes[j], 4 + j))
        turn[...] = homes[j][...].astype(f32).reshape(turn.shape)
        for k in range(SUB):
            cols = slice((j * SUB + k) * LANES, (j * SUB + k + 1) * LANES)
            out_ref[:, cols] = (
                turn[pl.ds(k, rows, stride=SUB), :] * gate_ref[:, cols]
            ).astype(bf16)


def local(
    tile_embed, destination, slide_lengths, w_inner, w_gate, conv_weight, conv_bias, x_project,
    dt_project, dt_bias, decay, skip_gain,
):
    shards = lax.axis_size(AXES)
    rows, model = tile_embed.shape
    width = w_inner.shape[1]
    states = decay.shape[1]
    rank = dt_project.shape[1]
    taps = conv_weight.shape[1]
    folds = width // LANES
    per_peer = rows // shards
    chunk = min(shards, rows)
    split = shards // (2 * states)
    halo = taps - 1
    me = lax.axis_index(AXES).astype(jnp.int32)
    me_arr = me[None]
    f32, bf16 = jnp.float32, jnp.bfloat16
    vmem = pl.BlockSpec(memory_space=pltpu.VMEM)
    smem = pl.BlockSpec(memory_space=pltpu.SMEM)
    params = pltpu.CompilerParams(vmem_limit_bytes=60 * 1024 * 1024)

    any_space = pl.BlockSpec(memory_space=pl.ANY)
    mfolds = model // LANES
    groups = 8
    fast = (
        shards == 2 * states and shards % groups == 0 and folds == 3 * SUB
        and states % (shards // groups) == 0 and (per_peer * mfolds) % 16 == 0
        and (per_peer * SUB) % 16 == 0
    )

    def remote_params(number):
        return pltpu.CompilerParams(
            vmem_limit_bytes=60 * 1024 * 1024, collective_id=number, has_side_effects=True
        )

    if fast:
        lane = jnp.arange(rows, dtype=jnp.int32)[None, :]
        slots = jnp.tile((destination % rows).astype(f32).reshape(shards, per_peer), (1, shards))
        slots = jnp.where(lane // per_peer == me, slots, 0.0)[:, None, :]
        sent_rows = pltpu.VMEM((shards, per_peer * mfolds, LANES), bf16)
        cell = pltpu.VMEM((shards, 2 * SUB, LANES), bf16)
        third = pltpu.VMEM((shards, per_peer * SUB, LANES), bf16)
        return pl.pallas_call(
            functools.partial(layer_kernel, shards, states, rank, chunk, groups),
            out_shape=jax.ShapeDtypeStruct((rows, width), bf16),
            in_specs=[smem] + [vmem] * 6 + [any_space] * 5,
            out_specs=vmem,
            scratch_shapes=[
                pltpu.VMEM((rows * mfolds, LANES), f32),
                sent_rows, sent_rows,
                pltpu.VMEM((shards, 1, rows), f32),
                pltpu.VMEM((rows, model), bf16),
                pltpu.VMEM((model, width), bf16),
                pltpu.VMEM((model, width), bf16),
                pltpu.VMEM(x_project.shape, bf16),
                pltpu.VMEM(dt_project.shape, bf16),
                pltpu.VMEM(decay.shape, f32),
                pltpu.VMEM((rows, width), bf16),
                pltpu.VMEM((2 * SUB, width), bf16),
                pltpu.VMEM((2 * SUB, width), bf16),
                pltpu.VMEM((rows, width), f32),
                pltpu.VMEM((rows, rows), bf16),
                pltpu.VMEM((2, folds, LANES), f32),
                pltpu.VMEM((2, rows * folds, LANES), f32),
                pltpu.VMEM((2 * rows, LANES), f32),
                pltpu.VMEM((rows * folds, LANES), f32),
                pltpu.VMEM((rows + 2 * SUB, width), f32),
                pltpu.VMEM((2, rows * folds, LANES), f32),
                pltpu.VMEM((2 * states * folds, LANES), f32),
                pltpu.VMEM((rows, width), bf16),
                pltpu.VMEM(((states + 1) * folds, LANES), f32),
                pltpu.SMEM((2 * rows, LANES), f32),
                pltpu.SemaphoreType.DMA,
                pltpu.VMEM((shards * 2 * SUB, LANES), f32),
                pltpu.VMEM((shards, 2 * SUB, LANES), f32),
                pltpu.VMEM((shards, 2 * SUB, LANES), f32),
                cell, cell, cell, cell, cell, cell, cell, cell,
                pltpu.VMEM((states * folds, LANES), f32),
                pltpu.VMEM((states * folds, LANES), f32),
                pltpu.VMEM((rows * SUB, LANES), f32),
                third, third, third, third, third, third,
                pltpu.SemaphoreType.DMA((9,)),
                pltpu.SemaphoreType.DMA((9,)),
                pltpu.SemaphoreType.DMA((2,)),
                pltpu.SemaphoreType.DMA((2,)),
                pltpu.SemaphoreType.DMA((5,)),
            ],
            compiler_params=remote_params(2),
            name="layer",
        )(
            slide_lengths, tile_embed, slots, conv_weight, conv_bias, dt_bias, skip_gain,
            w_gate, w_inner, x_project, dt_project, decay,
        )
    slot_col = jnp.broadcast_to((destination % rows).astype(bf16)[:, None], (rows, LANES))
    sent = jnp.concatenate([tile_embed, slot_col], axis=1).reshape(shards, per_peer, model + LANES)
    got = lax.all_to_all(sent, AXES, split_axis=0, concat_axis=0, tiled=True)
    got = got.reshape(rows, model + LANES)
    slot = got[:, model].astype(jnp.int32)
    place = (slot[None, :] == jnp.arange(rows, dtype=jnp.int32)[:, None]).astype(bf16)
    ordered = jnp.dot(place, got[:, :model], preferred_element_type=f32).astype(bf16)
    inner = jnp.dot(ordered, w_inner, preferred_element_type=f32).astype(bf16)
    up = [(i, i + 1) for i in range(shards - 1)]
    down = [(i + 1, i) for i in range(shards - 1)]
    before = lax.ppermute(inner[rows - 2 * SUB :], AXES, up)
    after = lax.ppermute(inner[: 2 * SUB], AXES, down)
    dt, proj, y, pay = pl.pallas_call(
        functools.partial(sweep_kernel, states, rank, chunk),
        out_shape=(
            jax.ShapeDtypeStruct((2, rows * folds, LANES), f32),
            jax.ShapeDtypeStruct((2 * rows, LANES), f32),
            jax.ShapeDtypeStruct((rows * folds, LANES), f32),
            jax.ShapeDtypeStruct((2 * states, 2 * folds, LANES), bf16),
        ),
        in_specs=[smem, smem] + [vmem] * 10,
        out_specs=(vmem,) * 4,
        scratch_shapes=[
            pltpu.VMEM((rows + 2 * SUB, width), f32),
            pltpu.VMEM((2, rows * folds, LANES), f32),
            pltpu.VMEM((2 * states * folds, LANES), f32),
            pltpu.VMEM((rows, width), bf16),
            pltpu.VMEM((2 * states, 2 * folds, LANES), f32),
            pltpu.SMEM((2 * rows, LANES), f32),
            pltpu.SemaphoreType.DMA,
        ],
        compiler_params=params,
        name="sweep",
    )(
        me_arr, slide_lengths, inner, before, after, conv_weight, conv_bias,
        x_project, dt_project, dt_bias, decay,
        skip_gain.reshape(2, folds, LANES),
    )
    pay = pay.reshape(2 * states, 2, split, folds // split, LANES)
    pay = pay.swapaxes(1, 2).reshape(shards, 2 * folds // split, LANES)
    theirs = lax.all_to_all(pay, AXES, split_axis=0, concat_axis=0, tiled=True)
    my_rate = lax.dynamic_slice_in_dim(
        decay.reshape(shards, folds // split, LANES), me, 1, axis=0
    )[0]
    enter = pl.pallas_call(
        functools.partial(relay_kernel, states, split, rows, chunk),
        out_shape=jax.ShapeDtypeStruct((shards, folds // split, LANES), bf16),
        in_specs=[smem, smem, vmem, vmem],
        out_specs=vmem,
        compiler_params=params,
        name="relay",
    )(me_arr, slide_lengths, theirs, my_rate)
    enter = lax.all_to_all(enter, AXES, split_axis=0, concat_axis=0, tiled=True)
    enter = enter.reshape(2 * states, folds, LANES)
    back = pl.pallas_call(
        functools.partial(finish_kernel, states, rank, chunk),
        out_shape=jax.ShapeDtypeStruct((rows * folds, LANES), bf16),
        in_specs=[smem, smem, smem] + [vmem] * 5,
        out_specs=vmem,
        scratch_shapes=[
            pltpu.VMEM((2 * states * folds, LANES), f32),
            pltpu.VMEM((rows * folds, LANES), f32),
        ],
        compiler_params=params,
        name="finish",
    )(
        me_arr, slide_lengths, proj, dt, y, enter, decay,
        place,
    )
    back = back.reshape(shards, per_peer, width)
    returned = lax.all_to_all(back, AXES, split_axis=0, concat_axis=0, tiled=True)
    gate = jnp.dot(tile_embed, w_gate, preferred_element_type=f32)
    return (returned.reshape(rows, width).astype(f32) * jax.nn.silu(gate)).astype(bf16)


def solution(mesh):
    placed = (P(AXES, None), P(AXES)) + (P(),) * 10
    return jax.shard_map(
        local, mesh=mesh, in_specs=placed, out_specs=P(AXES, None), check_vma=False
    )
```

```python
import functools

import jax
import jax.numpy as jnp
from jax import lax
from jax.experimental import pallas as pl
from jax.experimental.pallas import tpu as pltpu
from jax.sharding import PartitionSpec as P

AXES = ("seq", "slide")
LANES = 128
SUB = 8
LOG2E = 1.4426950408889634


def slide_starts(len_ref):
    starts = [jnp.int32(0)]
    for s in range(len_ref.shape[0]):
        starts.append(starts[-1] + len_ref[s])
    return starts


def keep_at(starts, pos):
    hit = pos == starts[0]
    for s in starts[1:]:
        hit = jnp.logical_or(hit, pos == s)
    return jnp.where(hit, 0.0, 1.0).astype(jnp.float32)


def spread_rates(decay_ref, rate_scr, folds):
    count = decay_ref.shape[1]
    for d in range(2):
        for k in range(folds):
            rate_scr[pl.ds(d * count * folds + k, count, stride=folds), :] = (
                decay_ref[d, :, k * LANES : (k + 1) * LANES] * -LOG2E
            )


def prepare(
    rank, starts, base, inner_ref, prev_ref, next_ref, cw_ref, cb_ref, xp_ref, dp_ref, db_ref,
    dt_ref, proj_ref, pad, u_ref, ubf, bc, sem,
):
    rows, width = inner_ref.shape
    folds = width // LANES
    taps = cw_ref.shape[1]
    halo = prev_ref.shape[0]
    pad[0:SUB, :] = prev_ref[halo - SUB :, :].astype(jnp.float32)
    pad[SUB : SUB + rows, :] = inner_ref[...].astype(jnp.float32)
    pad[SUB + rows : 2 * SUB + rows, :] = next_ref[0:SUB, :].astype(jnp.float32)
    where_at = base + lax.broadcasted_iota(jnp.int32, (rows, LANES), 0)
    masks = {}
    for dist in range(1, taps):
        for sign in (-1, 1):
            bad = jnp.zeros((rows, LANES), jnp.bool_)
            for s in starts:
                if sign < 0:
                    bad = bad | ((where_at - dist < s) & (where_at >= s))
                else:
                    bad = bad | ((where_at < s) & (where_at + dist >= s))
            masks[sign * dist] = jnp.where(bad, 0.0, 1.0)
    block = LANES
    wide = 2 * LANES
    for d in range(2):
        acc = jnp.zeros((rows, LANES), jnp.float32)
        for cb in range(width // wide):
            for half in range(2):
                k = 2 * cb + half
                cols = slice(k * block, (k + 1) * block)
                total = jnp.broadcast_to(cb_ref[d : d + 1, cols], (rows, block))
                for tap in range(taps):
                    dist = (tap - (taps - 1)) if d == 0 else (taps - 1 - tap)
                    term = pad[SUB + dist : SUB + dist + rows, cols]
                    if dist != 0:
                        term = term * masks[dist]
                    total = total + cw_ref[d, tap : tap + 1, cols] * term
                u = (total / (1.0 + jnp.exp(-total))).astype(jnp.bfloat16)
                ubf[:, cols] = u
                u_ref[d, pl.ds(k, rows, stride=folds), :] = u.astype(jnp.float32)
            wcols = slice(cb * wide, (cb + 1) * wide)
            acc = acc + jnp.dot(
                ubf[:, wcols], xp_ref[d, wcols, :], preferred_element_type=jnp.float32
            )
        proj_ref[d * rows : (d + 1) * rows, :] = acc
        low = acc[:, :rank].astype(jnp.bfloat16)
        for cb in range(width // wide):
            wcols = slice(cb * wide, (cb + 1) * wide)
            v = jnp.dot(low, dp_ref[d, :, wcols], preferred_element_type=jnp.float32)
            v = v + db_ref[d : d + 1, wcols]
            step = jnp.maximum(v, 0.0) + jnp.log1p(jnp.exp(-jnp.abs(v)))
            for half in range(2):
                dt_ref[d, pl.ds(2 * cb + half, rows, stride=folds), :] = step[
                    :, half * LANES : (half + 1) * LANES
                ]
    copy = pltpu.make_async_copy(proj_ref, bc, sem)
    copy.start()
    copy.wait()


def sweep_one(d, states, rank, chunk, rows, folds, starts, base, rate_scr, skip_ref, dt_ref, u_ref, bc, y_ref, keep_last, parts_of=None):
    chunks = rows // chunk
    zero = jnp.zeros((SUB, LANES), jnp.float32)
    if True:
        for j in range(folds // SUB) if parts_of is None else parts_of:
            rates = [
                rate_scr[(d * states + n) * folds + j * SUB : (d * states + n) * folds + (j + 1) * SUB, :]
                for n in range(states)
            ]
            skip = skip_ref[d, j * SUB : (j + 1) * SUB, :]

            def chunk_step(ci, carry):
                hs, sdt = carry
                c = ci if d == 0 else chunks - 1 - ci
                keep = keep_at(starts, base + (c if d == 0 else c + 1) * chunk)
                hs = tuple(h * keep for h in hs)

                def row_step(i, inner_carry):
                    hs, sdt = inner_carry
                    t = c * chunk + (i if d == 0 else chunk - 1 - i)
                    spot = pl.ds(pl.multiple_of(t * folds + j * SUB, SUB), SUB)
                    dt = dt_ref[d, spot, :]
                    u = u_ref[d, spot, :]
                    dtu = dt * u
                    parts = [skip * u, None, None, None]
                    out = []
                    for n in range(states):
                        h = jnp.exp2(dt * rates[n]) * hs[n] + dtu * bc[d * rows + t, rank + n]
                        out.append(h)
                        term = h * bc[d * rows + t, rank + states + n]
                        q = n % 4
                        parts[q] = term if parts[q] is None else parts[q] + term
                    y = (parts[0] + parts[1]) + (parts[2] + parts[3])
                    if d == 0:
                        y_ref[spot, :] = y
                    else:
                        y_ref[spot, :] += y
                    return (tuple(out), sdt + dt)

                return lax.fori_loop(0, chunk, row_step, (hs, sdt), unroll=16)

            hs, sdt = lax.fori_loop(0, chunks, chunk_step, ((zero,) * states, zero))
            keep_last(j, hs, sdt)


def sweep_kernel(
    states, rank, chunk,
    me_ref, len_ref, inner_ref, prev_ref, next_ref, cw_ref, cb_ref, xp_ref, dp_ref, db_ref,
    decay_ref, skip_ref,
    dt_ref, proj_ref, y_ref, pay_ref,
    pad, u_ref, rate_scr, ubf, held, bc, sem,
):
    rows, width = inner_ref.shape
    folds = width // LANES
    starts = slide_starts(len_ref)
    base = me_ref[0] * rows
    spread_rates(decay_ref, rate_scr, folds)
    prepare(
        rank, starts, base, inner_ref, prev_ref, next_ref, cw_ref, cb_ref, xp_ref, dp_ref, db_ref,
        dt_ref, proj_ref, pad, u_ref, ubf, bc, sem,
    )
    for d in range(2):

        def keep_last(j, hs, sdt):
            for n in range(states):
                held[d * states + n, j * SUB : (j + 1) * SUB, :] = hs[n]
                held[d * states + n, folds + j * SUB : folds + (j + 1) * SUB, :] = sdt

        sweep_one(
            d, states, rank, chunk, rows, folds, starts, base, rate_scr, skip_ref, dt_ref, u_ref,
            bc, y_ref, keep_last,
        )
    pay_ref[...] = held[...].astype(jnp.bfloat16)


def relay_kernel(states, split, rows, chunk, me_ref, len_ref, got_ref, rate_ref, out_ref):
    shards = got_ref.shape[0]
    depth = got_ref.shape[1] // 2
    starts = slide_starts(len_ref)
    backward = me_ref[0] // split >= states
    rate = rate_ref[...] * -LOG2E

    def step(i, h):
        s = jnp.where(backward, shards - 1 - i, i)
        keep = jnp.float32(1.0)
        for c in range(rows // chunk):
            keep = keep * keep_at(
                starts, s * rows + c * chunk + jnp.where(backward, chunk, 0)
            )
        out_ref[s] = h.astype(jnp.bfloat16)
        got = got_ref[s].astype(jnp.float32)
        return jnp.exp2(rate * got[depth:]) * (h * keep) + got[:depth]

    lax.fori_loop(0, shards, step, jnp.zeros((depth, LANES), jnp.float32))


def finish_one(d, j, states, rank, chunk, rows, folds, starts, base, rate_scr, enter_of, dt_ref, bc, y_ref, tot):
    chunks = rows // chunk
    rates = [
        rate_scr[(d * states + n) * folds + j * SUB : (d * states + n) * folds + (j + 1) * SUB, :]
        for n in range(states)
    ]
    enters = [
        enter_of(n)
        for n in range(states)
    ]

    def chunk_step(ci, carry):
        alive, sdt = carry
        c = ci if d == 0 else chunks - 1 - ci
        alive = alive * keep_at(starts, base + (c if d == 0 else c + 1) * chunk)

        def row_step(i, sdt):
            t = c * chunk + (i if d == 0 else chunk - 1 - i)
            spot = pl.ds(pl.multiple_of(t * folds + j * SUB, SUB), SUB)
            sdt = sdt + dt_ref[d, spot, :]
            parts = [None] * 4
            for n in range(states):
                term = jnp.exp2(sdt * rates[n]) * (
                    enters[n] * bc[d * rows + t, rank + states + n]
                )
                q = n % 4
                parts[q] = term if parts[q] is None else parts[q] + term
            y = ((parts[0] + parts[1]) + (parts[2] + parts[3])) * alive
            if d == 0:
                tot[spot, :] = y_ref[spot, :] + y
            else:
                tot[spot, :] += y
            return sdt

        return (alive, lax.fori_loop(0, chunk, row_step, sdt, unroll=16))

    lax.fori_loop(
        0, chunks, chunk_step, (jnp.float32(1.0), jnp.zeros((SUB, LANES), jnp.float32))
    )


def finish_kernel(
    states, rank, chunk,
    me_ref, len_ref, bc, dt_ref, y_ref, enter_ref, decay_ref, place_ref,
    out_ref,
    rate_scr, tot,
):
    rows = place_ref.shape[0]
    folds = decay_ref.shape[2] // LANES
    starts = slide_starts(len_ref)
    base = me_ref[0] * rows
    spread_rates(decay_ref, rate_scr, folds)
    for d in range(2):
        for j in range(folds // SUB):

            def enter_of(n):
                return enter_ref[d * states + n, j * SUB : (j + 1) * SUB, :].astype(jnp.float32)

            finish_one(
                d, j, states, rank, chunk, rows, folds, starts, base, rate_scr, enter_of, dt_ref,
                bc, y_ref, tot,
            )
    pick = place_ref[...]
    for k in range(folds):
        part = tot[pl.ds(k, rows, stride=folds), :].astype(jnp.bfloat16)
        tot[pl.ds(k, rows, stride=folds), :] = lax.dot_general(
            pick, part, (((0,), (0,)), ((), ())), preferred_element_type=jnp.float32
        )
    out_ref[...] = tot[...].astype(jnp.bfloat16)


def peer_id(peer):
    count = lax.axis_size("slide")
    return {"seq": lax.div(peer, count), "slide": lax.rem(peer, count)}


def greet_all(shards, me):
    barrier = pltpu.get_barrier_semaphore()

    def greet(i, _):
        pl.semaphore_signal(
            barrier, inc=1, device_id=peer_id(lax.rem(me + i, shards)),
            device_id_type=pl.DeviceIdType.MESH,
        )
        return 0

    lax.fori_loop(1, shards, greet, 0, unroll=True)


def await_all(shards):
    pl.semaphore_wait(pltpu.get_barrier_semaphore(), shards - 1)


def start_blocks(src, dst, me, shards, send_sem, recv_sem):
    def go(i, _):
        peer = lax.rem(me + i, shards)
        pltpu.make_async_remote_copy(
            src_ref=src.at[peer], dst_ref=dst.at[me], send_sem=send_sem, recv_sem=recv_sem,
            device_id=peer_id(peer), device_id_type=pl.DeviceIdType.MESH,
        ).start()
        return 0

    lax.fori_loop(1, shards, go, 0, unroll=True)


def await_blocks(src, dst, me, shards, send_sem, recv_sem):
    others = pl.ds(0, shards - 1)
    pltpu.make_async_remote_copy(
        src_ref=src.at[others], dst_ref=dst.at[others], send_sem=send_sem, recv_sem=recv_sem,
        device_id=peer_id(lax.rem(me + 1, shards)), device_id_type=pl.DeviceIdType.MESH,
    ).wait()


def layer_kernel(
    shards, states, rank, chunk, groups,
    len_ref, emb_ref, slots_ref, cw_ref, cb_ref, db_ref, skip_ref,
    wg_ref, wi_ref, xp_hbm, dp_hbm, decay_hbm,
    out_ref,
    scr, send, got, gslot, ordered, wg, wi, xp_ref, dp_ref, decay_ref,
    inner_ref, prev_ref, next_ref, gate_ref, place_ref, skip_scr,
    dt_ref, proj_ref, y_ref, pad, u_ref, rate_scr, ubf, held, bc, sem,
    stage, gotf, passes, pay0, pay1, got0, got1, ent0, ent1, land0, land1, enters0, enters1,
    turn, back0, back1, back2, home0, home1, home2, send_sem, recv_sem, halo_send, halo_recv,
    load_sem,
):
    rows, width = inner_ref.shape
    model = emb_ref.shape[1]
    folds = width // LANES
    mfolds = model // LANES
    wide = 2 * LANES
    edge = prev_ref.shape[0]
    per = folds // groups
    quads = shards // groups
    some = states // quads
    tall = some * per
    me = lax.axis_index(AXES)
    pays, gots, ents, lands = (pay0, pay1), (got0, got1), (ent0, ent1), (land0, land1)
    backs, homes = (back0, back1, back2), (home0, home1, home2)
    enters = (enters0, enters1)
    f32, bf16 = jnp.float32, jnp.bfloat16

    def route(src, dst, number):
        return (src, dst, me, shards, send_sem.at[number], recv_sem.at[number])

    greet_all(shards, me)
    pairs = ((wg_ref, wg), (decay_hbm, decay_ref), (wi_ref, wi), (xp_hbm, xp_ref), (dp_hbm, dp_ref))
    loads = [
        pltpu.make_async_copy(src, dst, load_sem.at[i]) for i, (src, dst) in enumerate(pairs)
    ]
    for load in loads:
        load.start()
    for k in range(mfolds):
        scr[pl.ds(k, rows, stride=mfolds), :] = emb_ref[:, k * LANES : (k + 1) * LANES].astype(f32)
    send[...] = scr[...].astype(bf16).reshape(send.shape)
    await_all(shards)
    start_blocks(*route(slots_ref, gslot, 7))
    start_blocks(*route(send, got, 8))
    got[me] = send[me]
    gslot[me] = slots_ref[me]
    starts = slide_starts(len_ref)
    base = me * rows
    for k in range(folds):
        for d in range(2):
            skip_scr[d, k : k + 1, :] = skip_ref[d : d + 1, k * LANES : (k + 1) * LANES]
    stage[...] = jnp.zeros(stage.shape, f32)
    passes[...] = jnp.zeros(passes.shape, f32)
    loads[0].wait()

    def gate_tile(cb, _):
        cols = pl.ds(pl.multiple_of(cb * wide, wide), wide)
        v = jnp.dot(emb_ref[...], wg[:, cols], preferred_element_type=f32)
        gate_ref[:, cols] = v / (1.0 + jnp.exp(-v))
        return 0

    lax.fori_loop(0, width // wide, gate_tile, 0)
    loads[1].wait()
    spread_rates(decay_ref, rate_scr, folds)
    for load in loads[2:]:
        load.wait()
    await_blocks(*route(slots_ref, gslot, 7))
    await_blocks(*route(send, got, 8))
    slot_row = jnp.sum(gslot[...], axis=0)
    place = (
        jnp.broadcast_to(slot_row, (rows, rows))
        == lax.broadcasted_iota(jnp.int32, (rows, rows), 0).astype(f32)
    ).astype(bf16)
    place_ref[...] = place
    scr[...] = got[...].astype(f32).reshape(scr.shape)
    for k in range(mfolds):
        ordered[:, k * LANES : (k + 1) * LANES] = jnp.dot(
            place, scr[pl.ds(k, rows, stride=mfolds), :].astype(bf16), preferred_element_type=f32
        ).astype(bf16)

    def inner_tile(cb, _):
        cols = pl.ds(pl.multiple_of(cb * wide, wide), wide)
        inner_ref[:, cols] = jnp.dot(
            ordered[...], wi[:, cols], preferred_element_type=f32
        ).astype(bf16)
        return 0

    lax.fori_loop(0, width // wide, inner_tile, 0)
    to_next = pltpu.make_async_remote_copy(
        src_ref=inner_ref.at[pl.ds(rows - edge, edge)], dst_ref=prev_ref,
        send_sem=halo_send.at[0], recv_sem=halo_recv.at[0],
        device_id=peer_id(lax.rem(me + 1, shards)), device_id_type=pl.DeviceIdType.MESH,
    )
    to_prev = pltpu.make_async_remote_copy(
        src_ref=inner_ref.at[pl.ds(0, edge)], dst_ref=next_ref,
        send_sem=halo_send.at[1], recv_sem=halo_recv.at[1],
        device_id=peer_id(lax.rem(me + shards - 1, shards)), device_id_type=pl.DeviceIdType.MESH,
    )
    to_next.start()
    to_prev.start()
    to_next.wait()
    to_prev.wait()
    prepare(
        rank, starts, base, inner_ref, prev_ref, next_ref, cw_ref, cb_ref, xp_ref, dp_ref, db_ref,
        dt_ref, proj_ref, pad, u_ref, ubf, bc, sem,
    )

    def keep_last(j, hs, sdt):
        for n in range(states):
            held[n * folds + j * SUB : n * folds + (j + 1) * SUB, :] = hs[n]
        held[states * folds + j * SUB : states * folds + (j + 1) * SUB, :] = sdt

    def sweep(d, parts_of):
        sweep_one(
            d, states, rank, chunk, rows, folds, starts, base, rate_scr, skip_scr, dt_ref, u_ref,
            bc, y_ref, keep_last, parts_of,
        )

    def pack(d):
        for g in range(groups):
            for q in range(quads):
                spot = (g * quads + q) * 2 * SUB
                for m in range(some):
                    row = (q * some + m) * folds + g * per
                    stage[spot + m * per : spot + (m + 1) * per, :] = held[row : row + per, :]
                row = states * folds + g * per
                stage[spot + tall : spot + tall + per, :] = held[row : row + per, :]
        pays[d][...] = stage[...].astype(bf16).reshape(pays[d].shape)

    def launch(d):
        start_blocks(*route(pays[d], gots[d], d))
        gots[d][me] = pays[d][me]

    def relay(d):
        await_blocks(*route(pays[d], gots[d], d))
        gotf[...] = gots[d][...].astype(f32)
        for m in range(some):
            row = (d * states + lax.rem(me, quads) * some + m) * folds + lax.div(me, quads) * per
            for f in range(per):
                rate = rate_scr[pl.ds(row + f, 1), :]
                passes[:, m * per + f : m * per + f + 1, :] = jnp.exp2(
                    rate[None] * gotf[:, tall + f : tall + f + 1, :]
                )

        def step(i, h):
            s = i if d == 0 else shards - 1 - i
            keep = jnp.float32(1.0)
            for c in range(rows // chunk):
                keep = keep * keep_at(starts, s * rows + c * chunk + d * chunk)
            ents[d][s] = h.astype(bf16)
            return passes[s] * (h * keep) + gotf[s]

        lax.fori_loop(0, shards, step, jnp.zeros((2 * SUB, LANES), f32), unroll=4)
        start_blocks(*route(ents[d], lands[d], 2 + d))
        lands[d][me] = ents[d][me]

    def arrive(d):
        await_blocks(*route(ents[d], lands[d], 2 + d))
        gotf[...] = lands[d][...].astype(f32)
        for g in range(groups):
            for q in range(quads):
                for m in range(some):
                    row = (q * some + m) * folds + g * per
                    enters[d][row : row + per, :] = gotf[g * quads + q, m * per : (m + 1) * per, :]

    def finish(d, j):
        def enter_of(n):
            return enters[d][n * folds + j * SUB : n * folds + (j + 1) * SUB, :]

        finish_one(
            d, j, states, rank, chunk, rows, folds, starts, base, rate_scr, enter_of, dt_ref, bc,
            y_ref, y_ref,
        )

    def give(j):
        for k in range(SUB):
            part = y_ref[pl.ds(j * SUB + k, rows, stride=folds), :].astype(bf16)
            turn[pl.ds(k, rows, stride=SUB), :] = lax.dot_general(
                place_ref[...], part, (((0,), (0,)), ((), ())), preferred_element_type=f32
            )
        backs[j][...] = turn[...].astype(bf16).reshape(backs[j].shape)
        start_blocks(*route(backs[j], homes[j], 4 + j))
        homes[j][me] = backs[j][me]

    sweep(0, (0, 1, 2))
    pack(0)
    launch(0)
    sweep(1, (0, 1))
    relay(0)
    sweep(1, (2,))
    pack(1)
    launch(1)
    arrive(0)
    finish(0, 0)
    relay(1)
    finish(0, 1)
    arrive(1)
    finish(1, 0)
    give(0)
    finish(1, 1)
    give(1)
    finish(0, 2)
    finish(1, 2)
    give(2)
    for j in range(folds // SUB):
        await_blocks(*route(backs[j], homes[j], 4 + j))
        turn[...] = homes[j][...].astype(f32).reshape(turn.shape)
        for k in range(SUB):
            cols = slice((j * SUB + k) * LANES, (j * SUB + k + 1) * LANES)
            out_ref[:, cols] = (
                turn[pl.ds(k, rows, stride=SUB), :] * gate_ref[:, cols]
            ).astype(bf16)


def local(
    tile_embed, destination, slide_lengths, w_inner, w_gate, conv_weight, conv_bias, x_project,
    dt_project, dt_bias, decay, skip_gain,
):
    shards = lax.axis_size(AXES)
    rows, model = tile_embed.shape
    width = w_inner.shape[1]
    states = decay.shape[1]
    rank = dt_project.shape[1]
    taps = conv_weight.shape[1]
    folds = width // LANES
    per_peer = rows // shards
    chunk = min(shards, rows)
    split = shards // (2 * states)
    halo = taps - 1
    me = lax.axis_index(AXES).astype(jnp.int32)
    me_arr = me[None]
    f32, bf16 = jnp.float32, jnp.bfloat16
    vmem = pl.BlockSpec(memory_space=pltpu.VMEM)
    smem = pl.BlockSpec(memory_space=pltpu.SMEM)
    params = pltpu.CompilerParams(vmem_limit_bytes=60 * 1024 * 1024)

    any_space = pl.BlockSpec(memory_space=pl.ANY)
    mfolds = model // LANES
    groups = 8
    fast = (
        shards == 2 * states and shards % groups == 0 and folds == 3 * SUB
        and states % (shards // groups) == 0 and (per_peer * mfolds) % 16 == 0
        and (per_peer * SUB) % 16 == 0
    )

    def remote_params(number):
        return pltpu.CompilerParams(
            vmem_limit_bytes=60 * 1024 * 1024, collective_id=number, has_side_effects=True
        )

    if fast:
        lane = jnp.arange(rows, dtype=jnp.int32)[None, :]
        slots = jnp.tile((destination % rows).astype(f32).reshape(shards, per_peer), (1, shards))
        slots = jnp.where(lane // per_peer == me, slots, 0.0)[:, None, :]
        sent_rows = pltpu.VMEM((shards, per_peer * mfolds, LANES), bf16)
        cell = pltpu.VMEM((shards, 2 * SUB, LANES), bf16)
        third = pltpu.VMEM((shards, per_peer * SUB, LANES), bf16)
        return pl.pallas_call(
            functools.partial(layer_kernel, shards, states, rank, chunk, groups),
            out_shape=jax.ShapeDtypeStruct((rows, width), bf16),
            in_specs=[smem] + [vmem] * 6 + [any_space] * 5,
            out_specs=vmem,
            scratch_shapes=[
                pltpu.VMEM((rows * mfolds, LANES), f32),
                sent_rows, sent_rows,
                pltpu.VMEM((shards, 1, rows), f32),
                pltpu.VMEM((rows, model), bf16),
                pltpu.VMEM((model, width), bf16),
                pltpu.VMEM((model, width), bf16),
                pltpu.VMEM(x_project.shape, bf16),
                pltpu.VMEM(dt_project.shape, bf16),
                pltpu.VMEM(decay.shape, f32),
                pltpu.VMEM((rows, width), bf16),
                pltpu.VMEM((2 * SUB, width), bf16),
                pltpu.VMEM((2 * SUB, width), bf16),
                pltpu.VMEM((rows, width), f32),
                pltpu.VMEM((rows, rows), bf16),
                pltpu.VMEM((2, folds, LANES), f32),
                pltpu.VMEM((2, rows * folds, LANES), f32),
                pltpu.VMEM((2 * rows, LANES), f32),
                pltpu.VMEM((rows * folds, LANES), f32),
                pltpu.VMEM((rows + 2 * SUB, width), f32),
                pltpu.VMEM((2, rows * folds, LANES), f32),
                pltpu.VMEM((2 * states * folds, LANES), f32),
                pltpu.VMEM((rows, width), bf16),
                pltpu.VMEM(((states + 1) * folds, LANES), f32),
                pltpu.SMEM((2 * rows, LANES), f32),
                pltpu.SemaphoreType.DMA,
                pltpu.VMEM((shards * 2 * SUB, LANES), f32),
                pltpu.VMEM((shards, 2 * SUB, LANES), f32),
                pltpu.VMEM((shards, 2 * SUB, LANES), f32),
                cell, cell, cell, cell, cell, cell, cell, cell,
                pltpu.VMEM((states * folds, LANES), f32),
                pltpu.VMEM((states * folds, LANES), f32),
                pltpu.VMEM((rows * SUB, LANES), f32),
                third, third, third, third, third, third,
                pltpu.SemaphoreType.DMA((9,)),
                pltpu.SemaphoreType.DMA((9,)),
                pltpu.SemaphoreType.DMA((2,)),
                pltpu.SemaphoreType.DMA((2,)),
                pltpu.SemaphoreType.DMA((5,)),
            ],
            compiler_params=remote_params(2),
            name="layer",
        )(
            slide_lengths, tile_embed, slots, conv_weight, conv_bias, dt_bias, skip_gain,
            w_gate, w_inner, x_project, dt_project, decay,
        )
    slot_col = jnp.broadcast_to((destination % rows).astype(bf16)[:, None], (rows, LANES))
    sent = jnp.concatenate([tile_embed, slot_col], axis=1).reshape(shards, per_peer, model + LANES)
    got = lax.all_to_all(sent, AXES, split_axis=0, concat_axis=0, tiled=True)
    got = got.reshape(rows, model + LANES)
    slot = got[:, model].astype(jnp.int32)
    place = (slot[None, :] == jnp.arange(rows, dtype=jnp.int32)[:, None]).astype(bf16)
    ordered = jnp.dot(place, got[:, :model], preferred_element_type=f32).astype(bf16)
    inner = jnp.dot(ordered, w_inner, preferred_element_type=f32).astype(bf16)
    up = [(i, i + 1) for i in range(shards - 1)]
    down = [(i + 1, i) for i in range(shards - 1)]
    before = lax.ppermute(inner[rows - 2 * SUB :], AXES, up)
    after = lax.ppermute(inner[: 2 * SUB], AXES, down)
    dt, proj, y, pay = pl.pallas_call(
        functools.partial(sweep_kernel, states, rank, chunk),
        out_shape=(
            jax.ShapeDtypeStruct((2, rows * folds, LANES), f32),
            jax.ShapeDtypeStruct((2 * rows, LANES), f32),
            jax.ShapeDtypeStruct((rows * folds, LANES), f32),
            jax.ShapeDtypeStruct((2 * states, 2 * folds, LANES), bf16),
        ),
        in_specs=[smem, smem] + [vmem] * 10,
        out_specs=(vmem,) * 4,
        scratch_shapes=[
            pltpu.VMEM((rows + 2 * SUB, width), f32),
            pltpu.VMEM((2, rows * folds, LANES), f32),
            pltpu.VMEM((2 * states * folds, LANES), f32),
            pltpu.VMEM((rows, width), bf16),
            pltpu.VMEM((2 * states, 2 * folds, LANES), f32),
            pltpu.SMEM((2 * rows, LANES), f32),
            pltpu.SemaphoreType.DMA,
        ],
        compiler_params=params,
        name="sweep",
    )(
        me_arr, slide_lengths, inner, before, after, conv_weight, conv_bias,
        x_project, dt_project, dt_bias, decay,
        skip_gain.reshape(2, folds, LANES),
    )
    pay = pay.reshape(2 * states, 2, split, folds // split, LANES)
    pay = pay.swapaxes(1, 2).reshape(shards, 2 * folds // split, LANES)
    theirs = lax.all_to_all(pay, AXES, split_axis=0, concat_axis=0, tiled=True)
    my_rate = lax.dynamic_slice_in_dim(
        decay.reshape(shards, folds // split, LANES), me, 1, axis=0
    )[0]
    enter = pl.pallas_call(
        functools.partial(relay_kernel, states, split, rows, chunk),
        out_shape=jax.ShapeDtypeStruct((shards, folds // split, LANES), bf16),
        in_specs=[smem, smem, vmem, vmem],
        out_specs=vmem,
        compiler_params=params,
        name="relay",
    )(me_arr, slide_lengths, theirs, my_rate)
    enter = lax.all_to_all(enter, AXES, split_axis=0, concat_axis=0, tiled=True)
    enter = enter.reshape(2 * states, folds, LANES)
    back = pl.pallas_call(
        functools.partial(finish_kernel, states, rank, chunk),
        out_shape=jax.ShapeDtypeStruct((rows * folds, LANES), bf16),
        in_specs=[smem, smem, smem] + [vmem] * 5,
        out_specs=vmem,
        scratch_shapes=[
            pltpu.VMEM((2 * states * folds, LANES), f32),
            pltpu.VMEM((rows * folds, LANES), f32),
        ],
        compiler_params=params,
        name="finish",
    )(
        me_arr, slide_lengths, proj, dt, y, enter, decay,
        place,
    )
    back = back.reshape(shards, per_peer, width)
    returned = lax.all_to_all(back, AXES, split_axis=0, concat_axis=0, tiled=True)
    gate = jnp.dot(tile_embed, w_gate, preferred_element_type=f32)
    return (returned.reshape(rows, width).astype(f32) * jax.nn.silu(gate)).astype(bf16)


def solution(mesh):
    placed = (P(AXES, None), P(AXES)) + (P(),) * 10
    return jax.shard_map(
        local, mesh=mesh, in_specs=placed, out_specs=P(AXES, None), check_vma=False
    )
```
